32 devices in a mesh: space: 8 (over z, x), tm: 4 (over y, core).
Axes of the slice: x: 2, y: 2, z: 4, core: 2. Of those that a mesh axis runs over, the one named last changes fastest.
Arguments:
- snapshots: bfloat16 [81920, 2048], P('space', 'tm'), may hold values from -6 to 6
- modes: bfloat16 [81920, 256], P('space'), may hold values from -0.01953125 to 0.01953125
Outputs:
- gram: float32 [4864, 4864], P('tm', 'space')
- rhs: float32 [4864, 256], P('tm', 'space')
The draws below stay inside these ranges and needn't reach their ends.
All inputs are finite; a program needn't handle non-finite values.
Results may differ from the reference program's by a relative error of at most 0.0057.
Values may be sent and summed in bfloat16 or wider, within the bound.
No kernel may reach another device: no remote copies, remote signals or barrier semaphores. Data moves between devices by JAX's collectives and lax.ppermute only.
A program may use at most 128 MiB of HBM per device.

```python
import jax
import jax.numpy as jnp
from jax import lax

BASIS_MODES = 256
LEAD_MODES = 48
SNAP_DEV = 512
FEATURES = 4864
DELAY_GAP = 512
DOF_TOTAL = 81920
SNAPSHOTS = 2048
N_TM = 4


def block_levels(rng, extent, split, smallest, top_value):
    def one(axis_at, parts):
        steps = jax.random.uniform(jax.random.fold_in(jax.random.fold_in(rng, 6), axis_at), (parts,), jnp.float32, smallest / len(split), top_value / len(split))
        return jnp.repeat(jnp.exp(steps), extent[axis_at] // parts).reshape((-1,) + (1,) * (len(extent) - axis_at - 1))

    loudness = one(*split[0])
    for cut in split[1:]:
        loudness = loudness * one(*cut)
    return loudness


def bell_draw(own_key, shape, spread, reach, split=(), held_as=jnp.bfloat16):
    array = spread * jax.random.normal(own_key, shape, jnp.float32)
    if split:
        array = array * block_levels(own_key, shape, split, -0.22, 0.18)
    return jnp.clip(array, -reach, reach).astype(held_as)


def setup_inputs(seed: int = 0) -> dict:
    key_list = jax.random.split(jax.random.key(seed), 3)
    return {
        "snapshots": bell_draw(key_list[0], (DOF_TOTAL, SNAPSHOTS), 1.0, 6.0, ((0, 8), (1, 4))),
        "modes": bell_draw(key_list[1], (DOF_TOTAL, BASIS_MODES), DOF_TOTAL ** -0.5, 0.01953125, ((0, 8),)),
    }


def build_features(current, first, second):
    steps_count = current.shape[1]
    lead = first.shape[0]
    head = current[0:lead].astype(jnp.float32)
    prod_one = (head[:, None, :] * first.astype(jnp.float32)[None, :, :]).reshape(lead * lead, steps_count)
    prod_two = (head[:, None, :] * second.astype(jnp.float32)[None, :, :]).reshape(lead * lead, steps_count)
    return jnp.concatenate([current.astype(jnp.float32), prod_one, prod_two], axis=0).astype(jnp.bfloat16)


def reference(snapshots, modes):
    def project(block_id):
        start = (block_id * SNAP_DEV).astype(jnp.int32)
        piece = lax.dynamic_slice_in_dim(snapshots, start, SNAP_DEV, 1)
        return lax.dot_general(modes, piece, (((0,), (0,)), ((), ())), preferred_element_type=jnp.float32)

    blocks = lax.map(project, jnp.arange(N_TM, dtype=jnp.int32))
    coeffs = jnp.concatenate([blocks[k] for k in range(N_TM)], axis=1).astype(jnp.bfloat16)
    lead = coeffs[0:LEAD_MODES]
    first = jnp.pad(lead, ((0, 0), (DELAY_GAP, 0)))[:, 0:SNAPSHOTS]
    second = jnp.pad(lead, ((0, 0), (2 * DELAY_GAP, 0)))[:, 0:SNAPSHOTS]
    target = jnp.pad(coeffs, ((0, 0), (0, DELAY_GAP)))[:, DELAY_GAP:]
    phi = build_features(coeffs, first, second)
    gram = jnp.dot(phi, phi.T, preferred_element_type=jnp.float32) / SNAPSHOTS + 0.05 * jnp.eye(FEATURES, dtype=jnp.float32)
    rhs = jnp.dot(phi, target.T, preferred_element_type=jnp.float32) / SNAPSHOTS
    return gram, rhs
```

```python
import functools

import jax
import jax.numpy as jnp
from jax import lax
from jax.experimental import pallas as pl
from jax.experimental.pallas import tpu as pltpu
from jax.sharding import PartitionSpec as P

LEAD_MODES = 48
RIDGE_WEIGHT = 0.05
ROW_TILE = 16


def swap(value, axis, bit):
    count = lax.axis_size(axis)
    return lax.ppermute(value, axis, [(i, i ^ bit) for i in range(count)])


def bits_of(count):
    return [1 << k for k in range(count.bit_length() - 1)]


def gram_kernel(
    sizes, pos_ref, lead_ref, rest_ref, gram_ref, rhs_ref, delayed, head, rows, cols, side
):
    n_time, snaps, modes, row_block, col_block, target_block = sizes
    total = n_time * snaps
    time_pos, space_pos = pos_ref[0], pos_ref[1]

    def slot(block):
        return jnp.bitwise_xor(time_pos, block)

    def window(block):
        return pl.ds(block * snaps, snaps)

    nothing = jnp.zeros((LEAD_MODES, snaps), jnp.bfloat16)
    for block in range(n_time):
        current = lead_ref[slot(block)]
        head[:, window(block)] = current.astype(jnp.float32)
        for delay in (1, 2):
            if block + delay < n_time:
                delayed[delay - 1, :, window(block + delay)] = current
            if block < delay:
                delayed[delay - 1, :, window(block)] = nothing

    def fill(out, start, extent):
        @pl.when(start == 0)
        def _():
            for block in range(n_time):
                out[pl.ds(LEAD_MODES, LEAD_MODES), window(block)] = lead_ref[slot(block)]
                out[pl.ds(2 * LEAD_MODES, modes - LEAD_MODES), window(block)] = rest_ref[
                    slot(block)
                ]

        def group(q, carry):
            kind, i = lax.div(q, LEAD_MODES), lax.rem(q, LEAD_MODES)
            at = modes + LEAD_MODES * q - start + LEAD_MODES
            factor = jnp.broadcast_to(head[pl.ds(i, 1), :], (ROW_TILE, total)).astype(
                jnp.bfloat16
            )
            for j in range(0, LEAD_MODES, ROW_TILE):
                out[pl.ds(pl.multiple_of(at + j, ROW_TILE), ROW_TILE), :] = (
                    factor * delayed[kind, j : j + ROW_TILE, :]
                )
            return carry

        first = jnp.maximum(0, lax.div(start - modes, LEAD_MODES))
        last = lax.div(start + extent - modes + LEAD_MODES - 1, LEAD_MODES)
        lax.fori_loop(first, last, group, 0)

    fill(cols, space_pos * col_block, col_block)
    fill(rows, time_pos * row_block, row_block)
    wanted = space_pos * target_block
    for block in range(n_time):
        for j in range(0, target_block, ROW_TILE):
            out = cols.at[pl.ds(LEAD_MODES + col_block + j, ROW_TILE), window(block)]
            if block + 1 < n_time:
                mode = wanted + j

                @pl.when(mode < LEAD_MODES)
                def _():
                    out[...] = lead_ref[
                        slot(block + 1), pl.ds(pl.multiple_of(mode, ROW_TILE), ROW_TILE), :
                    ]

                @pl.when(mode >= LEAD_MODES)
                def _():
                    out[...] = rest_ref[
                        slot(block + 1),
                        pl.ds(pl.multiple_of(mode - LEAD_MODES, ROW_TILE), ROW_TILE),
                        :,
                    ]
            else:
                out[...] = jnp.zeros((ROW_TILE, snaps), jnp.bfloat16)

    tile = row_block // 4 if row_block % (4 * ROW_TILE) == 0 else row_block

    def multiply(step, carry):
        top = pl.multiple_of(step * tile, ROW_TILE)
        product = (
            lax.dot_general(
                rows[pl.ds(LEAD_MODES + top, tile), :],
                cols[pl.ds(LEAD_MODES, col_block + target_block), :],
                (((1,), (1,)), ((), ())),
                preferred_element_type=jnp.float32,
            )
            / total
        )
        shape = (tile, col_block)
        row = time_pos * row_block + top + lax.broadcasted_iota(jnp.int32, shape, 0)
        column = space_pos * col_block + lax.broadcasted_iota(jnp.int32, shape, 1)
        gram_ref[pl.ds(top, tile), :] = product[:, 0:col_block] + jnp.where(
            row == column, RIDGE_WEIGHT, 0.0
        )
        side[pl.ds(top, tile), :] = product[:, col_block:]
        return carry

    lax.fori_loop(0, row_block // tile, multiply, 0)
    rhs_ref[...] = side[...].T


def gram_blocks(lead, rest, n_space):
    n_time, _, snaps = lead.shape
    modes = LEAD_MODES + rest.shape[1]
    features = modes + 2 * LEAD_MODES * LEAD_MODES
    row_block, col_block, target_block = features // n_time, features // n_space, modes // n_space
    total = n_time * snaps
    here = jnp.stack([lax.axis_index("tm"), lax.axis_index("space")]).astype(jnp.int32)
    vmem = pl.BlockSpec(memory_space=pltpu.VMEM)
    gram, rhs = pl.pallas_call(
        functools.partial(
            gram_kernel, (n_time, snaps, modes, row_block, col_block, target_block)
        ),
        out_shape=(
            jax.ShapeDtypeStruct((row_block, col_block), jnp.float32),
            jax.ShapeDtypeStruct((target_block, row_block), jnp.float32),
        ),
        in_specs=[pl.BlockSpec(memory_space=pltpu.SMEM), vmem, vmem],
        out_specs=(vmem, vmem),
        scratch_shapes=[
            pltpu.VMEM((2, LEAD_MODES, total), jnp.bfloat16),
            pltpu.VMEM((LEAD_MODES, total), jnp.float32),
            pltpu.VMEM((row_block + 2 * LEAD_MODES, total), jnp.bfloat16),
            pltpu.VMEM((col_block + 2 * LEAD_MODES + target_block, total), jnp.bfloat16),
            pltpu.VMEM((row_block, target_block), jnp.float32),
        ],
        compiler_params=pltpu.CompilerParams(vmem_limit_bytes=56 * 2**20),
    )(here, lead, rest)
    return gram, rhs.T


def per_device(snapshots, modes):
    n_space, n_time = lax.axis_size("space"), lax.axis_size("tm")
    partial_sums = lax.dot_general(
        modes, snapshots, (((0,), (0,)), ((), ())), preferred_element_type=jnp.float32
    )
    lead = partial_sums[0:LEAD_MODES]
    rest = partial_sums[LEAD_MODES:].astype(jnp.bfloat16)
    for bit in bits_of(n_space):
        lead = lead + swap(lead, "space", bit)
        arrived = swap(rest, "space", bit)
        rest = (rest.astype(jnp.float32) + arrived.astype(jnp.float32)).astype(jnp.bfloat16)
    lead = lead.astype(jnp.bfloat16)[None]
    rest = rest[None]
    for bit in reversed(bits_of(n_time)):
        lead = jnp.stack([lead, swap(lead, "tm", bit)], axis=1)
        lead = lead.reshape((-1,) + lead.shape[2:])
        rest = jnp.stack([rest, swap(rest, "tm", bit)], axis=1)
        rest = rest.reshape((-1,) + rest.shape[2:])
    return gram_blocks(lead, rest, n_space)


def solution(mesh):
    in_specs = (P("space", "tm"), P("space", None))
    out_specs = (P("tm", "space"), P("tm", "space"))
    return jax.shard_map(
        per_device, mesh=mesh, in_specs=in_specs, out_specs=out_specs, check_vma=False
    )
```

```python
import functools

import jax
import jax.numpy as jnp
from jax import lax
from jax.experimental import pallas as pl
from jax.experimental.pallas import tpu as pltpu
from jax.sharding import PartitionSpec as P

LEAD_MODES = 48
RIDGE_WEIGHT = 0.05
ROW_TILE = 16
QUAD = 4


def swap(value, axis, bit):
    count = lax.axis_size(axis)
    return lax.ppermute(value, axis, [(i, i ^ bit) for i in range(count)])


def bits_of(count):
    return [1 << k for k in range(count.bit_length() - 1)]


def gram_kernel(sizes, pos_ref, *refs):
    n_time, snaps, modes, row_block, col_block, target_block = sizes
    half, quarter = n_time // 2, snaps // QUAD
    lead_refs, rest_refs, (gram_ref, rhs_ref) = refs[0:2], refs[2 : 2 + 2 * QUAD], refs[10:12]
    delayed, head, rows, cols, side, rest = refs[12:]
    total = n_time * snaps
    time_pos, space_pos = pos_ref[0], pos_ref[1]
    core = lax.rem(time_pos, 2)
    place = lax.rem(space_pos, QUAD)

    def window(block):
        return pl.ds(pl.multiple_of(block * snaps, snaps), snaps)

    for other in range(2):
        for k in range(half):
            block = jnp.bitwise_xor(time_pos, 2 * k + other)
            current = lead_refs[other][k]
            head[:, window(block)] = current.astype(jnp.float32)
            for delay in (1, 2):

                @pl.when(block + delay < n_time)
                def _():
                    delayed[delay - 1, :, window(block + delay)] = current

            for j in range(QUAD):
                at = block * snaps + jnp.bitwise_xor(place, j) * quarter
                rest[:, pl.ds(pl.multiple_of(at, quarter), quarter)] = rest_refs[
                    other * QUAD + j
                ][k]
    for delay in (1, 2):
        delayed[delay - 1, :, 0 : delay * snaps] = jnp.zeros(
            (LEAD_MODES, delay * snaps), jnp.bfloat16
        )

    def fill(out, start, extent):
        @pl.when(start == 0)
        def _():
            out[pl.ds(LEAD_MODES, LEAD_MODES), :] = head[...].astype(jnp.bfloat16)
            out[pl.ds(2 * LEAD_MODES, modes - LEAD_MODES), :] = rest[...]

        def group(q, carry):
            kind, i = lax.div(q, LEAD_MODES), lax.rem(q, LEAD_MODES)
            at = modes + LEAD_MODES * q - start + LEAD_MODES
            factor = jnp.broadcast_to(head[pl.ds(i, 1), :], (ROW_TILE, total)).astype(
                jnp.bfloat16
            )
            for j in range(0, LEAD_MODES, ROW_TILE):
                out[pl.ds(pl.multiple_of(at + j, ROW_TILE), ROW_TILE), :] = (
                    factor * delayed[kind, j : j + ROW_TILE, :]
                )
            return carry

        first = jnp.maximum(0, lax.div(start - modes, LEAD_MODES))
        last = lax.div(start + extent - modes + LEAD_MODES - 1, LEAD_MODES)
        lax.fori_loop(first, last, group, 0)

    fill(cols, space_pos * col_block, col_block)
    fill(rows, time_pos * row_block, row_block)
    for j in range(0, target_block, ROW_TILE):
        out = cols.at[pl.ds(LEAD_MODES + col_block + j, ROW_TILE), :]
        mode = space_pos * target_block + j
        later = slice(snaps, total)

        @pl.when(mode < LEAD_MODES)
        def _():
            out[:, 0 : total - snaps] = head[
                pl.ds(pl.multiple_of(mode, ROW_TILE), ROW_TILE), later
            ].astype(jnp.bfloat16)

        @pl.when(mode >= LEAD_MODES)
        def _():
            out[:, 0 : total - snaps] = rest[
                pl.ds(pl.multiple_of(mode - LEAD_MODES, ROW_TILE), ROW_TILE), later
            ]

        out[:, total - snaps :] = jnp.zeros((ROW_TILE, snaps), jnp.bfloat16)

    tile = row_block // 4 if row_block % (4 * ROW_TILE) == 0 else row_block

    def multiply(step, carry):
        top = pl.multiple_of(step * tile, ROW_TILE)
        product = (
            lax.dot_general(
                rows[pl.ds(LEAD_MODES + top, tile), :],
                cols[pl.ds(LEAD_MODES, col_block + target_block), :],
                (((1,), (1,)), ((), ())),
                preferred_element_type=jnp.float32,
            )
            / total
        )
        shape = (tile, col_block)
        row = time_pos * row_block + top + lax.broadcasted_iota(jnp.int32, shape, 0)
        column = space_pos * col_block + lax.broadcasted_iota(jnp.int32, shape, 1)
        gram_ref[pl.ds(top, tile), :] = product[:, 0:col_block] + jnp.where(
            row == column, RIDGE_WEIGHT, 0.0
        )
        side[pl.ds(top, tile), :] = product[:, col_block:]
        return carry

    lax.fori_loop(0, row_block // tile, multiply, 0)
    rhs_ref[...] = side[...].T


def gram_blocks(lead, rest, n_time, n_space):
    _, lead_modes, snaps = lead[0].shape
    modes = lead_modes + rest[0].shape[1]
    features = modes + 2 * LEAD_MODES * LEAD_MODES
    row_block, col_block, target_block = features // n_time, features // n_space, modes // n_space
    total = n_time * snaps
    here = jnp.stack([lax.axis_index("tm"), lax.axis_index("space")]).astype(jnp.int32)
    vmem = pl.BlockSpec(memory_space=pltpu.VMEM)
    gram, rhs = pl.pallas_call(
        functools.partial(
            gram_kernel, (n_time, snaps, modes, row_block, col_block, target_block)
        ),
        out_shape=(
            jax.ShapeDtypeStruct((row_block, col_block), jnp.float32),
            jax.ShapeDtypeStruct((target_block, row_block), jnp.float32),
        ),
        in_specs=[pl.BlockSpec(memory_space=pltpu.SMEM)] + [vmem] * (2 + 2 * QUAD),
        out_specs=(vmem, vmem),
        scratch_shapes=[
            pltpu.VMEM((2, LEAD_MODES, total), jnp.bfloat16),
            pltpu.VMEM((LEAD_MODES, total), jnp.float32),
            pltpu.VMEM((row_block + 2 * LEAD_MODES, total), jnp.bfloat16),
            pltpu.VMEM((col_block + 2 * LEAD_MODES + target_block, total), jnp.bfloat16),
            pltpu.VMEM((row_block, target_block), jnp.float32),
            pltpu.VMEM((modes - lead_modes, total), jnp.bfloat16),
        ],
        compiler_params=pltpu.CompilerParams(vmem_limit_bytes=56 * 2**20),
    )(here, *lead, *rest)
    return gram, rhs.T


def to_sum(*parts):
    return functools.reduce(jnp.add, [part.astype(jnp.float32) for part in parts])


def joined(value, axis, bit):
    return jnp.concatenate([value, swap(value, axis, bit)], axis=0)


def per_device(snapshots, modes):
    n_space, n_time = lax.axis_size("space"), lax.axis_size("tm")
    partial_sums = lax.dot_general(
        modes, snapshots, (((0,), (0,)), ((), ())), preferred_element_type=jnp.float32
    )
    snaps = partial_sums.shape[1]
    quarter = snaps // QUAD
    place = lax.rem(lax.axis_index("space"), QUAD)
    lead = partial_sums[0:LEAD_MODES]
    rest = partial_sums[LEAD_MODES:]

    def quarter_of(j):
        start = jnp.bitwise_xor(place, j) * quarter
        return lax.dynamic_slice_in_dim(rest, start, quarter, 1)

    arrived = [
        swap(quarter_of(j).astype(jnp.bfloat16), "space", j) for j in range(1, QUAD)
    ]
    mine = to_sum(quarter_of(0), *arrived).astype(jnp.bfloat16)
    for bit in bits_of(n_space):
        lead = lead + swap(lead, "space", bit)
        if bit >= QUAD:
            mine = to_sum(mine, swap(mine, "space", bit)).astype(jnp.bfloat16)
    lead = lead.astype(jnp.bfloat16)[None]
    mine = mine[None]
    for bit in bits_of(n_time)[1:]:
        lead = joined(lead, "tm", bit)
        mine = joined(mine, "tm", bit)
    rest = [mine] + [swap(mine, "space", j) for j in range(1, QUAD)]
    lead = [lead, swap(lead, "tm", 1)]
    rest = rest + [swap(piece, "tm", 1) for piece in rest]
    return gram_blocks(lead, rest, n_time, n_space)


def solution(mesh):
    in_specs = (P("space", "tm"), P("space", None))
    out_specs = (P("tm", "space"), P("tm", "space"))
    return jax.shard_map(
        per_device, mesh=mesh, in_specs=in_specs, out_specs=out_specs, check_vma=False
    )
```

```python
import functools

import jax
import jax.numpy as jnp
from jax import lax
from jax.experimental import pallas as pl
from jax.experimental.pallas import tpu as pltpu
from jax.sharding import PartitionSpec as P

LEAD_MODES = 48
RIDGE_WEIGHT = 0.05
ROW_TILE = 16
QUAD = 4


def swap(value, axis, bit):
    count = lax.axis_size(axis)
    return lax.ppermute(value, axis, [(i, i ^ bit) for i in range(count)])


def bits_of(count):
    return [1 << k for k in range(count.bit_length() - 1)]


def gram_kernel(sizes, pos_ref, *refs):
    n_time, snaps, modes, row_block, col_block, target_block = sizes
    half, quarter = n_time // 2, snaps // QUAD
    pieces, (gram_ref, rhs_ref) = refs[0 : 2 * QUAD], refs[2 * QUAD : 2 * QUAD + 2]
    coeffs, delayed, head, rows, cols, side = refs[2 * QUAD + 2 :]
    total = n_time * snaps
    time_pos, space_pos = pos_ref[0], pos_ref[1]
    place = lax.rem(space_pos, QUAD)

    for other in range(2):
        for k in range(half):
            block = jnp.bitwise_xor(time_pos, 2 * k + other)
            for j in range(QUAD):
                at = block * snaps + jnp.bitwise_xor(place, j) * quarter
                coeffs[:, pl.ds(pl.multiple_of(at, quarter), quarter)] = pieces[
                    other * QUAD + j
                ][k]
    head[...] = coeffs[0:LEAD_MODES, :].astype(jnp.float32)
    for delay in (1, 2):
        gap = delay * snaps
        delayed[delay - 1, :, 0:gap] = jnp.zeros((LEAD_MODES, gap), jnp.bfloat16)
        delayed[delay - 1, :, gap:] = coeffs[0:LEAD_MODES, 0 : total - gap]

    def fill(out, start, extent):
        @pl.when(start == 0)
        def _():
            out[pl.ds(LEAD_MODES, modes), :] = coeffs[...]

        def group(q, carry):
            kind, i = lax.div(q, LEAD_MODES), lax.rem(q, LEAD_MODES)
            at = modes + LEAD_MODES * q - start + LEAD_MODES
            factor = jnp.broadcast_to(head[pl.ds(i, 1), :], (ROW_TILE, total)).astype(
                jnp.bfloat16
            )
            for j in range(0, LEAD_MODES, ROW_TILE):
                out[pl.ds(pl.multiple_of(at + j, ROW_TILE), ROW_TILE), :] = (
                    factor * delayed[kind, j : j + ROW_TILE, :]
                )
            return carry

        first = jnp.maximum(0, lax.div(start - modes, LEAD_MODES))
        last = lax.div(start + extent - modes + LEAD_MODES - 1, LEAD_MODES)
        lax.fori_loop(first, last, group, 0)

    fill(cols, space_pos * col_block, col_block)
    fill(rows, time_pos * row_block, row_block)
    wanted = pl.ds(pl.multiple_of(space_pos * target_block, ROW_TILE), target_block)
    at = pl.ds(LEAD_MODES + col_block, target_block)
    cols[at, 0 : total - snaps] = coeffs[wanted, snaps:]
    cols[at, total - snaps :] = jnp.zeros((target_block, snaps), jnp.bfloat16)

    tile = row_block // 4 if row_block % (4 * ROW_TILE) == 0 else row_block

    def multiply(step, carry):
        top = pl.multiple_of(step * tile, ROW_TILE)
        product = (
            lax.dot_general(
                rows[pl.ds(LEAD_MODES + top, tile), :],
                cols[pl.ds(LEAD_MODES, col_block + target_block), :],
                (((1,), (1,)), ((), ())),
                preferred_element_type=jnp.float32,
            )
            / total
        )
        shape = (tile, col_block)
        row = time_pos * row_block + top + lax.broadcasted_iota(jnp.int32, shape, 0)
        column = space_pos * col_block + lax.broadcasted_iota(jnp.int32, shape, 1)
        gram_ref[pl.ds(top, tile), :] = product[:, 0:col_block] + jnp.where(
            row == column, RIDGE_WEIGHT, 0.0
        )
        side[pl.ds(top, tile), :] = product[:, col_block:]
        return carry

    lax.fori_loop(0, row_block // tile, multiply, 0)
    rhs_ref[...] = side[...].T


def gram_blocks(pieces, n_time, n_space):
    half, modes, quarter = pieces[0].shape
    snaps = QUAD * quarter
    features = modes + 2 * LEAD_MODES * LEAD_MODES
    row_block, col_block, target_block = features // n_time, features // n_space, modes // n_space
    total = n_time * snaps
    here = jnp.stack([lax.axis_index("tm"), lax.axis_index("space")]).astype(jnp.int32)
    vmem = pl.BlockSpec(memory_space=pltpu.VMEM)
    gram, rhs = pl.pallas_call(
        functools.partial(
            gram_kernel, (n_time, snaps, modes, row_block, col_block, target_block)
        ),
        out_shape=(
            jax.ShapeDtypeStruct((row_block, col_block), jnp.float32),
            jax.ShapeDtypeStruct((target_block, row_block), jnp.float32),
        ),
        in_specs=[pl.BlockSpec(memory_space=pltpu.SMEM)] + [vmem] * (2 * QUAD),
        out_specs=(vmem, vmem),
        scratch_shapes=[
            pltpu.VMEM((modes, total), jnp.bfloat16),
            pltpu.VMEM((2, LEAD_MODES, total), jnp.bfloat16),
            pltpu.VMEM((LEAD_MODES, total), jnp.float32),
            pltpu.VMEM((row_block + 2 * LEAD_MODES, total), jnp.bfloat16),
            pltpu.VMEM((col_block + 2 * LEAD_MODES + target_block, total), jnp.bfloat16),
            pltpu.VMEM((row_block, target_block), jnp.float32),
        ],
        compiler_params=pltpu.CompilerParams(vmem_limit_bytes=56 * 2**20),
    )(here, *pieces)
    return gram, rhs.T


def rounded(value):
    high = lax.reduce_precision(value, 8, 7)
    left = value[0:LEAD_MODES] - high[0:LEAD_MODES]
    return jnp.concatenate([high, left], axis=0).astype(jnp.bfloat16)


def restored(value):
    modes = value.shape[0] - LEAD_MODES
    whole = value[0:modes].astype(jnp.float32)
    left = value[modes:].astype(jnp.float32)
    return jnp.concatenate([whole[0:LEAD_MODES] + left, whole[LEAD_MODES:]], axis=0)


def joined(value, axis, bit):
    return jnp.concatenate([value, swap(value, axis, bit)], axis=0)


def per_device(snapshots, modes):
    n_space, n_time = lax.axis_size("space"), lax.axis_size("tm")
    partial_sums = lax.dot_general(
        modes, snapshots, (((0,), (0,)), ((), ())), preferred_element_type=jnp.float32
    )
    snaps = partial_sums.shape[1]
    quarter = snaps // QUAD
    place = lax.rem(lax.axis_index("space"), QUAD)

    def quarter_of(j):
        start = jnp.bitwise_xor(place, j) * quarter
        return lax.dynamic_slice_in_dim(partial_sums, start, quarter, 1)

    arrived = [swap(rounded(quarter_of(j)), "space", j) for j in range(1, QUAD)]
    mine = quarter_of(0)
    for part in arrived:
        mine = mine + restored(part)
    for bit in bits_of(n_space)[2:]:
        sent = rounded(mine)
        mine = restored(sent) + restored(swap(sent, "space", bit))
    mine = mine.astype(jnp.bfloat16)[None]
    for bit in bits_of(n_time)[1:]:
        mine = joined(mine, "tm", bit)
    pieces = [mine] + [swap(mine, "space", j) for j in range(1, QUAD)]
    pieces = pieces + [swap(piece, "tm", 1) for piece in pieces]
    return gram_blocks(pieces, n_time, n_space)


def solution(mesh):
    in_specs = (P("space", "tm"), P("space", None))
    out_specs = (P("tm", "space"), P("tm", "space"))
    return jax.shard_map(
        per_device, mesh=mesh, in_specs=in_specs, out_specs=out_specs, check_vma=False
    )
```

```python
import functools

import jax
import jax.numpy as jnp
from jax import lax
from jax.experimental import pallas as pl
from jax.experimental.pallas import tpu as pltpu
from jax.sharding import PartitionSpec as P

LEAD_MODES = 48
RIDGE_WEIGHT = 0.05
ROW_TILE = 16
QUAD = 4
CUTS = (0, 112)


def swap(value, axis, bit):
    count = lax.axis_size(axis)
    return lax.ppermute(value, axis, [(i, i ^ bit) for i in range(count)])


def bits_of(count):
    return [1 << k for k in range(count.bit_length() - 1)]


def gram_kernel(sizes, pos_ref, *refs):
    n_time, snaps, modes, row_block, col_block, target_block = sizes
    half, quarter = n_time // 2, snaps // QUAD
    count = 2 * QUAD * len(CUTS)
    pieces, (gram_ref, rhs_ref) = refs[0:count], refs[count : count + 2]
    coeffs, delayed, head, rows, cols, side = refs[count + 2 :]
    total = n_time * snaps
    time_pos, space_pos = pos_ref[0], pos_ref[1]
    place = lax.rem(space_pos, QUAD)

    for other in range(2):
        for k in range(half):
            block = jnp.bitwise_xor(time_pos, 2 * k + other)
            for j in range(QUAD):
                at = block * snaps + jnp.bitwise_xor(place, j) * quarter
                at = pl.ds(pl.multiple_of(at, quarter), quarter)
                for cut, first in enumerate(CUTS):
                    piece = pieces[(cut * 2 + other) * QUAD + j]
                    coeffs[first : first + piece.shape[1], at] = piece[k]
    head[...] = coeffs[0:LEAD_MODES, :].astype(jnp.float32)
    for delay in (1, 2):
        gap = delay * snaps
        delayed[delay - 1, :, 0:gap] = jnp.zeros((LEAD_MODES, gap), jnp.bfloat16)
        delayed[delay - 1, :, gap:] = coeffs[0:LEAD_MODES, 0 : total - gap]

    def fill(out, start, extent):
        @pl.when(start == 0)
        def _():
            out[pl.ds(LEAD_MODES, modes), :] = coeffs[...]

        def group(q, carry):
            kind, i = lax.div(q, LEAD_MODES), lax.rem(q, LEAD_MODES)
            at = modes + LEAD_MODES * q - start + LEAD_MODES
            factor = jnp.broadcast_to(head[pl.ds(i, 1), :], (ROW_TILE, total)).astype(
                jnp.bfloat16
            )
            for j in range(0, LEAD_MODES, ROW_TILE):
                out[pl.ds(pl.multiple_of(at + j, ROW_TILE), ROW_TILE), :] = (
                    factor * delayed[kind, j : j + ROW_TILE, :]
                )
            return carry

        first = jnp.maximum(0, lax.div(start - modes, LEAD_MODES))
        last = lax.div(start + extent - modes + LEAD_MODES - 1, LEAD_MODES)
        lax.fori_loop(first, last, group, 0)

    fill(cols, space_pos * col_block, col_block)
    fill(rows, time_pos * row_block, row_block)
    wanted = pl.ds(pl.multiple_of(space_pos * target_block, ROW_TILE), target_block)
    at = pl.ds(LEAD_MODES + col_block, target_block)
    cols[at, 0 : total - snaps] = coeffs[wanted, snaps:]
    cols[at, total - snaps :] = jnp.zeros((target_block, snaps), jnp.bfloat16)

    tile = row_block // 4 if row_block % (4 * ROW_TILE) == 0 else row_block

    def multiply(step, carry):
        top = pl.multiple_of(step * tile, ROW_TILE)
        product = (
            lax.dot_general(
                rows[pl.ds(LEAD_MODES + top, tile), :],
                cols[pl.ds(LEAD_MODES, col_block + target_block), :],
                (((1,), (1,)), ((), ())),
                preferred_element_type=jnp.float32,
            )
            / total
        )
        shape = (tile, col_block)
        row = time_pos * row_block + top + lax.broadcasted_iota(jnp.int32, shape, 0)
        column = space_pos * col_block + lax.broadcasted_iota(jnp.int32, shape, 1)
        gram_ref[pl.ds(top, tile), :] = product[:, 0:col_block] + jnp.where(
            row == column, RIDGE_WEIGHT, 0.0
        )
        side[pl.ds(top, tile), :] = product[:, col_block:]
        return carry

    lax.fori_loop(0, row_block // tile, multiply, 0)
    rhs_ref[...] = side[...].T


def gram_blocks(pieces, n_time, n_space):
    quarter = pieces[0].shape[2]
    modes = sum(piece.shape[1] for piece in pieces) // (2 * QUAD)
    snaps = QUAD * quarter
    features = modes + 2 * LEAD_MODES * LEAD_MODES
    row_block, col_block, target_block = features // n_time, features // n_space, modes // n_space
    total = n_time * snaps
    here = jnp.stack([lax.axis_index("tm"), lax.axis_index("space")]).astype(jnp.int32)
    vmem = pl.BlockSpec(memory_space=pltpu.VMEM)
    gram, rhs = pl.pallas_call(
        functools.partial(
            gram_kernel, (n_time, snaps, modes, row_block, col_block, target_block)
        ),
        out_shape=(
            jax.ShapeDtypeStruct((row_block, col_block), jnp.float32),
            jax.ShapeDtypeStruct((target_block, row_block), jnp.float32),
        ),
        in_specs=[pl.BlockSpec(memory_space=pltpu.SMEM)] + [vmem] * len(pieces),
        out_specs=(vmem, vmem),
        scratch_shapes=[
            pltpu.VMEM((modes, total), jnp.bfloat16),
            pltpu.VMEM((2, LEAD_MODES, total), jnp.bfloat16),
            pltpu.VMEM((LEAD_MODES, total), jnp.float32),
            pltpu.VMEM((row_block + 2 * LEAD_MODES, total), jnp.bfloat16),
            pltpu.VMEM((col_block + 2 * LEAD_MODES + target_block, total), jnp.bfloat16),
            pltpu.VMEM((row_block, target_block), jnp.float32),
        ],
        compiler_params=pltpu.CompilerParams(vmem_limit_bytes=56 * 2**20),
    )(here, *pieces)
    return gram, rhs.T


def rounded(value, lead):
    high = lax.reduce_precision(value, 8, 7)
    left = value[0:lead] - high[0:lead]
    return jnp.concatenate([high, left], axis=0).astype(jnp.bfloat16)


def restored(value, lead):
    modes = value.shape[0] - lead
    whole = value[0:modes].astype(jnp.float32)
    left = value[modes:].astype(jnp.float32)
    return jnp.concatenate([whole[0:lead] + left, whole[lead:]], axis=0)


def joined(value, axis, bit):
    return jnp.concatenate([value, swap(value, axis, bit)], axis=0)


def gathered(partial_sums, lead):
    n_space, n_time = lax.axis_size("space"), lax.axis_size("tm")
    quarter = partial_sums.shape[1] // QUAD
    place = lax.rem(lax.axis_index("space"), QUAD)

    def quarter_of(j):
        start = jnp.bitwise_xor(place, j) * quarter
        return lax.dynamic_slice_in_dim(partial_sums, start, quarter, 1)

    arrived = [swap(rounded(quarter_of(j), lead), "space", j) for j in range(1, QUAD)]
    mine = quarter_of(0)
    for part in arrived:
        mine = mine + restored(part, lead)
    for bit in bits_of(n_space)[2:]:
        sent = rounded(mine, lead)
        mine = restored(sent, lead) + restored(swap(sent, "space", bit), lead)
    mine = mine.astype(jnp.bfloat16)[None]
    for bit in bits_of(n_time)[1:]:
        mine = joined(mine, "tm", bit)
    pieces = [mine] + [swap(mine, "space", j) for j in range(1, QUAD)]
    return pieces + [swap(piece, "tm", 1) for piece in pieces]


def per_device(snapshots, modes):
    partial_sums = lax.dot_general(
        modes, snapshots, (((0,), (0,)), ((), ())), preferred_element_type=jnp.float32
    )
    ends = CUTS[1:] + (modes.shape[1],)
    pieces = []
    for first, end in zip(CUTS, ends):
        pieces += gathered(partial_sums[first:end], LEAD_MODES if first == 0 else 0)
    return gram_blocks(pieces, lax.axis_size("tm"), lax.axis_size("space"))


def solution(mesh):
    in_specs = (P("space", "tm"), P("space", None))
    out_specs = (P("tm", "space"), P("tm", "space"))
    return jax.shard_map(
        per_device, mesh=mesh, in_specs=in_specs, out_specs=out_specs, check_vma=False
    )
```

```python
import functools

import jax
import jax.numpy as jnp
from jax import lax
from jax.experimental import pallas as pl
from jax.experimental.pallas import tpu as pltpu
from jax.sharding import PartitionSpec as P

LEAD_MODES = 48
RIDGE_WEIGHT = 0.05
ROW_TILE = 16
QUAD = 4
PROJECTION_STEPS = 10
VMEM_LIMIT = 48 * 2**20


def swap(value, axis, bit):
    count = lax.axis_size(axis)
    return lax.ppermute(value, axis, [(i, i ^ bit) for i in range(count)])


def bits_of(count):
    return [1 << k for k in range(count.bit_length() - 1)]


def in_vmem(value):
    return pltpu.with_memory_space_constraint(value, pltpu.VMEM)


def rounded(value):
    high = lax.reduce_precision(value, 8, 7)
    left = value[0:LEAD_MODES] - high[0:LEAD_MODES]
    return jnp.concatenate([high, left], axis=0).astype(jnp.bfloat16)


def restored(value):
    modes = value.shape[0] - LEAD_MODES
    whole = value[0:modes].astype(jnp.float32)
    left = value[modes:].astype(jnp.float32)
    return jnp.concatenate([whole[0:LEAD_MODES] + left, whole[LEAD_MODES:]], axis=0)


def projection_kernel(modes_hbm, snaps_hbm, own_ref, *refs):
    sent_refs, (modes, snaps, partial_sums, modes_sems, snaps_sems) = refs[0:3], refs[3:]
    depth = modes.shape[0] // PROJECTION_STEPS
    quarter = snaps.shape[1] // QUAD

    def copies(step):
        at = pl.ds(step * depth, depth)
        return (
            pltpu.make_async_copy(modes_hbm.at[at], modes.at[at], modes_sems.at[step]),
            pltpu.make_async_copy(snaps_hbm.at[at], snaps.at[at], snaps_sems.at[step]),
        )

    for step in range(PROJECTION_STEPS):
        for copy in copies(step):
            copy.start()
    for step in range(PROJECTION_STEPS):
        for copy in copies(step):
            copy.wait()
        at = pl.ds(step * depth, depth)
        product = lax.dot_general(
            modes[at, :],
            snaps[at, :],
            (((0,), (0,)), ((), ())),
            preferred_element_type=jnp.float32,
        )
        if step == 0:
            partial_sums[...] = product
        else:
            partial_sums[...] += product
    place = lax.rem(lax.axis_index("space"), QUAD)
    count = partial_sums.shape[0]
    for j in range(QUAD):
        start = pl.multiple_of(jnp.bitwise_xor(place, j) * quarter, quarter)
        part = partial_sums[:, pl.ds(start, quarter)]
        if j == 0:
            own_ref[...] = part
        else:
            high = part.astype(jnp.bfloat16)
            left = part[0:LEAD_MODES] - high[0:LEAD_MODES].astype(jnp.float32)
            sent_refs[j - 1][0:count, :] = high
            sent_refs[j - 1][count:, :] = left.astype(jnp.bfloat16)


def project(modes, snapshots):
    (depth, count), snaps = modes.shape, snapshots.shape[1]
    quarter = snaps // QUAD
    vmem = pl.BlockSpec(memory_space=pltpu.VMEM)
    anywhere = pl.BlockSpec(memory_space=pl.ANY)
    own, *sent = pl.pallas_call(
        projection_kernel,
        out_shape=(pltpu.VMEM((count, quarter), jnp.float32),)
        + (pltpu.VMEM((count + LEAD_MODES, quarter), jnp.bfloat16),) * (QUAD - 1),
        in_specs=[anywhere] * 2,
        out_specs=(vmem,) * QUAD,
        scratch_shapes=[
            pltpu.VMEM((depth, count), jnp.bfloat16),
            pltpu.VMEM((depth, snaps), jnp.bfloat16),
            pltpu.VMEM((count, snaps), jnp.float32),
            pltpu.SemaphoreType.DMA((PROJECTION_STEPS,)),
            pltpu.SemaphoreType.DMA((PROJECTION_STEPS,)),
        ],
        compiler_params=pltpu.CompilerParams(vmem_limit_bytes=VMEM_LIMIT),
        cost_estimate=pl.CostEstimate(
            flops=2 * depth * count * snaps,
            bytes_accessed=2 * depth * (count + snaps),
            transcendentals=0,
        ),
    )(modes, snapshots)
    return own, sent


def gram_kernel(sizes, *refs):
    n_time, snaps, modes, row_block, col_block, target_block, tile = sizes
    half, quarter = n_time // 2, snaps // QUAD
    count = 2 * QUAD
    pieces, (gram_hbm, rhs_ref) = refs[0:count], refs[count : count + 2]
    delayed, head, rows, cols, staged, sems = refs[count + 2 :]
    total = n_time * snaps
    time_pos, space_pos = lax.axis_index("tm"), lax.axis_index("space")
    place = lax.rem(space_pos, QUAD)

    def each_piece(take):
        for other in range(2):
            for k in range(half):
                block = jnp.bitwise_xor(time_pos, 2 * k + other)
                for j in range(QUAD):
                    within = jnp.bitwise_xor(place, j) * quarter
                    take(pieces[other * QUAD + j].at[k], block, within)

    def quarter_at(block, within):
        return pl.ds(pl.multiple_of(block * snaps + within, quarter), quarter)

    for delay in (1, 2):
        gap = delay * snaps
        delayed[delay - 1, :, 0:gap] = jnp.zeros((LEAD_MODES, gap), jnp.bfloat16)

    wanted = pl.ds(pl.multiple_of(space_pos * target_block, ROW_TILE), target_block)
    targets = pl.ds(LEAD_MODES + col_block, target_block)
    cols[targets, total - snaps :] = jnp.zeros((target_block, snaps), jnp.bfloat16)

    def place_lead(piece, block, within):
        current = piece[0:LEAD_MODES, :]
        head[:, quarter_at(block, within)] = current.astype(jnp.float32)
        for delay in (1, 2):

            @pl.when(block + delay < n_time)
            def _():
                delayed[delay - 1, :, quarter_at(block + delay, within)] = current

        @pl.when(block >= 1)
        def _():
            cols[targets, quarter_at(block - 1, within)] = piece[wanted, :]

    each_piece(place_lead)

    def fill(out, start, extent):
        @pl.when(start == 0)
        def _():
            def place_modes(piece, block, within):
                out[pl.ds(LEAD_MODES, modes), quarter_at(block, within)] = piece[...]

            each_piece(place_modes)

        def group(q, carry):
            kind, i = lax.div(q, LEAD_MODES), lax.rem(q, LEAD_MODES)
            at = modes + LEAD_MODES * q - start + LEAD_MODES
            factor = jnp.broadcast_to(head[pl.ds(i, 1), :], (ROW_TILE, total)).astype(
                jnp.bfloat16
            )
            for j in range(0, LEAD_MODES, ROW_TILE):
                out[pl.ds(pl.multiple_of(at + j, ROW_TILE), ROW_TILE), :] = (
                    factor * delayed[kind, j : j + ROW_TILE, :]
                )
            return carry

        first = jnp.maximum(0, lax.div(start - modes, LEAD_MODES))
        last = lax.div(start + extent - modes + LEAD_MODES - 1, LEAD_MODES)
        lax.fori_loop(first, last, group, 0)

    kept = cols[targets, :]
    fill(cols, space_pos * col_block, col_block)
    cols[targets, :] = kept
    fill(rows, time_pos * row_block, row_block)

    writes = []
    for step in range(row_block // tile):
        top = step * tile
        product = lax.dot_general(
            rows[pl.ds(LEAD_MODES + top, tile), :],
            cols[pl.ds(LEAD_MODES, col_block + target_block), :],
            (((1,), (1,)), ((), ())),
            preferred_element_type=jnp.float32,
        ) * (1.0 / total)
        shape = (tile, col_block)
        row = time_pos * row_block + top + lax.broadcasted_iota(jnp.int32, shape, 0)
        column = space_pos * col_block + lax.broadcasted_iota(jnp.int32, shape, 1)
        staged[pl.ds(top, tile), :] = product[:, 0:col_block] + jnp.where(
            row == column, RIDGE_WEIGHT, 0.0
        )
        at = pl.ds(top, tile)
        writes.append(pltpu.make_async_copy(staged.at[at], gram_hbm.at[at], sems.at[step]))
        writes[-1].start()
        rhs_ref[:, top : top + tile] = product[:, col_block:].T
    for write in writes:
        write.wait()


def gram_blocks(pieces, n_time, n_space):
    _, modes, quarter = pieces[0].shape
    snaps = QUAD * quarter
    features = modes + 2 * LEAD_MODES * LEAD_MODES
    row_block, col_block, target_block = features // n_time, features // n_space, modes // n_space
    total = n_time * snaps
    tile = row_block // 2 if row_block % (2 * ROW_TILE) == 0 else row_block
    vmem = pl.BlockSpec(memory_space=pltpu.VMEM)
    gram, rhs = pl.pallas_call(
        functools.partial(
            gram_kernel, (n_time, snaps, modes, row_block, col_block, target_block, tile)
        ),
        out_shape=(
            jax.ShapeDtypeStruct((row_block, col_block), jnp.float32),
            jax.ShapeDtypeStruct((target_block, row_block), jnp.float32),
        ),
        in_specs=[vmem] * len(pieces),
        out_specs=(pl.BlockSpec(memory_space=pl.ANY), vmem),
        scratch_shapes=[
            pltpu.VMEM((2, LEAD_MODES, total), jnp.bfloat16),
            pltpu.VMEM((LEAD_MODES, total), jnp.float32),
            pltpu.VMEM((row_block + 2 * LEAD_MODES, total), jnp.bfloat16),
            pltpu.VMEM((col_block + 2 * LEAD_MODES + target_block, total), jnp.bfloat16),
            pltpu.VMEM((row_block, col_block), jnp.float32),
            pltpu.SemaphoreType.DMA((row_block // tile,)),
        ],
        compiler_params=pltpu.CompilerParams(vmem_limit_bytes=VMEM_LIMIT),
        cost_estimate=pl.CostEstimate(
            flops=2 * row_block * (col_block + target_block) * total,
            bytes_accessed=4 * row_block * (col_block + target_block),
            transcendentals=0,
        ),
    )(*map(in_vmem, pieces))
    return gram, rhs.T


def joined(value, axis, bit):
    return jnp.concatenate([value, swap(value, axis, bit)], axis=0)


def per_device(snapshots, modes):
    n_space, n_time = lax.axis_size("space"), lax.axis_size("tm")
    mine, sent = project(modes, snapshots)
    arrived = [swap(part, "space", j) for j, part in enumerate(sent, 1)]
    for part in arrived:
        mine = mine + restored(part)
    for bit in bits_of(n_space)[2:]:
        out = rounded(mine)
        mine = restored(out) + restored(swap(out, "space", bit))
    mine = mine.astype(jnp.bfloat16)[None]
    for bit in bits_of(n_time)[1:]:
        mine = joined(mine, "tm", bit)
    pieces = [mine] + [swap(mine, "space", j) for j in range(1, QUAD)]
    pieces = pieces + [swap(piece, "tm", 1) for piece in pieces]
    return gram_blocks(pieces, n_time, n_space)


def solution(mesh):
    in_specs = (P("space", "tm"), P("space", None))
    out_specs = (P("tm", "space"), P("tm", "space"))
    return jax.shard_map(
        per_device, mesh=mesh, in_specs=in_specs, out_specs=out_specs, check_vma=False
    )
```

```python
import functools

import jax
import jax.numpy as jnp
from jax import lax
from jax.experimental import pallas as pl
from jax.experimental.pallas import tpu as pltpu
from jax.sharding import PartitionSpec as P

LEAD_MODES = 48
RIDGE_WEIGHT = 0.05
ROW_TILE = 16
QUAD = 4
PROJECTION_STEPS = 10
VMEM_LIMIT = 48 * 2**20


def swap(value, axis, bit):
    count = lax.axis_size(axis)
    return lax.ppermute(value, axis, [(i, i ^ bit) for i in range(count)])


def bits_of(count):
    return [1 << k for k in range(count.bit_length() - 1)]


def in_hbm(value):
    return pltpu.with_memory_space_constraint(value, pltpu.HBM)


def in_vmem(value):
    return pltpu.with_memory_space_constraint(value, pltpu.VMEM)


def rounded(value):
    high = lax.reduce_precision(value, 8, 7)
    left = value[0:LEAD_MODES] - high[0:LEAD_MODES]
    return jnp.concatenate([high, left], axis=0).astype(jnp.bfloat16)


def restored(value):
    modes = value.shape[0] - LEAD_MODES
    whole = value[0:modes].astype(jnp.float32)
    left = value[modes:].astype(jnp.float32)
    return jnp.concatenate([whole[0:LEAD_MODES] + left, whole[LEAD_MODES:]], axis=0)


def projection_kernel(modes_hbm, snaps_hbm, own_ref, *refs):
    sent_refs, (modes, snaps, partial_sums, modes_sems, snaps_sems) = refs[0:3], refs[3:]
    depth = modes.shape[0] // PROJECTION_STEPS
    quarter = snaps.shape[1] // QUAD

    def copies(step):
        at = pl.ds(step * depth, depth)
        return (
            pltpu.make_async_copy(modes_hbm.at[at], modes.at[at], modes_sems.at[step]),
            pltpu.make_async_copy(snaps_hbm.at[at], snaps.at[at], snaps_sems.at[step]),
        )

    for step in range(PROJECTION_STEPS):
        for copy in copies(step):
            copy.start()
    for step in range(PROJECTION_STEPS):
        for copy in copies(step):
            copy.wait()
        at = pl.ds(step * depth, depth)
        product = lax.dot_general(
            modes[at, :],
            snaps[at, :],
            (((0,), (0,)), ((), ())),
            preferred_element_type=jnp.float32,
        )
        if step == 0:
            partial_sums[...] = product
        else:
            partial_sums[...] += product
    place = lax.rem(lax.axis_index("space"), QUAD)
    count = partial_sums.shape[0]
    for j in range(QUAD):
        start = pl.multiple_of(jnp.bitwise_xor(place, j) * quarter, quarter)
        part = partial_sums[:, pl.ds(start, quarter)]
        if j == 0:
            own_ref[...] = part
        else:
            high = part.astype(jnp.bfloat16)
            left = part[0:LEAD_MODES] - high[0:LEAD_MODES].astype(jnp.float32)
            sent_refs[j - 1][0:count, :] = high
            sent_refs[j - 1][count:, :] = left.astype(jnp.bfloat16)


def project(modes, snapshots):
    (depth, count), snaps = modes.shape, snapshots.shape[1]
    quarter = snaps // QUAD
    vmem = pl.BlockSpec(memory_space=pltpu.VMEM)
    anywhere = pl.BlockSpec(memory_space=pltpu.HBM)
    own, *sent = pl.pallas_call(
        projection_kernel,
        out_shape=(pltpu.VMEM((count, quarter), jnp.float32),)
        + (pltpu.VMEM((count + LEAD_MODES, quarter), jnp.bfloat16),) * (QUAD - 1),
        in_specs=[anywhere] * 2,
        out_specs=(vmem,) * QUAD,
        scratch_shapes=[
            pltpu.VMEM((depth, count), jnp.bfloat16),
            pltpu.VMEM((depth, snaps), jnp.bfloat16),
            pltpu.VMEM((count, snaps), jnp.float32),
            pltpu.SemaphoreType.DMA((PROJECTION_STEPS,)),
            pltpu.SemaphoreType.DMA((PROJECTION_STEPS,)),
        ],
        compiler_params=pltpu.CompilerParams(vmem_limit_bytes=VMEM_LIMIT),
        cost_estimate=pl.CostEstimate(
            flops=2 * depth * count * snaps,
            bytes_accessed=2 * depth * (count + snaps),
            transcendentals=0,
        ),
    )(in_hbm(modes), in_hbm(snapshots))
    return own, sent


def gram_kernel(sizes, *refs):
    n_time, snaps, modes, row_block, col_block, target_block, tile = sizes
    half, quarter = n_time // 2, snaps // QUAD
    count = 2 * QUAD
    pieces, (gram_hbm, rhs_ref) = refs[0:count], refs[count : count + 2]
    delayed, head, rows, cols, opening, opening_target, staged, side, sems = refs[count + 2 :]
    later = (n_time - 1) * snaps
    time_pos, space_pos = lax.axis_index("tm"), lax.axis_index("space")
    place = lax.rem(space_pos, QUAD)

    def each_piece(take):
        for other in range(2):
            for k in range(half):
                block = jnp.bitwise_xor(time_pos, 2 * k + other)
                for j in range(QUAD):
                    within = pl.multiple_of(jnp.bitwise_xor(place, j) * quarter, quarter)
                    take(pieces[other * QUAD + j].at[k], block, within)

    def later_at(block, within):
        return pl.ds(pl.multiple_of((block - 1) * snaps + within, quarter), quarter)

    delayed[1, :, 0:snaps] = jnp.zeros((LEAD_MODES, snaps), jnp.bfloat16)
    wanted = pl.ds(pl.multiple_of(space_pos * target_block, ROW_TILE), target_block)
    targets = pl.ds(LEAD_MODES + col_block, target_block)

    def place_lead(piece, block, within):
        current = piece[0:LEAD_MODES, :]

        @pl.when(block >= 1)
        def _():
            head[:, later_at(block, within)] = current.astype(jnp.float32)

        for delay in (1, 2):

            @pl.when(block + delay < n_time)
            def _():
                delayed[delay - 1, :, later_at(block + delay, within)] = current

    each_piece(place_lead)

    def fill(out, start, extent):
        @pl.when(start == 0)
        def _():
            def place_modes(piece, block, within):
                @pl.when(block >= 1)
                def _():
                    out[pl.ds(LEAD_MODES, modes), later_at(block, within)] = piece[...]

            each_piece(place_modes)

        def group(q, carry):
            kind, i = lax.div(q, LEAD_MODES), lax.rem(q, LEAD_MODES)
            at = modes + LEAD_MODES * q - start + LEAD_MODES
            factor = jnp.broadcast_to(head[pl.ds(i, 1), :], (ROW_TILE, later)).astype(
                jnp.bfloat16
            )
            for j in range(0, LEAD_MODES, ROW_TILE):
                out[pl.ds(pl.multiple_of(at + j, ROW_TILE), ROW_TILE), :] = (
                    factor * delayed[kind, j : j + ROW_TILE, :]
                )
            return carry

        first = jnp.maximum(0, lax.div(start - modes, LEAD_MODES))
        last = lax.div(start + extent - modes + LEAD_MODES - 1, LEAD_MODES)
        lax.fori_loop(first, last, group, 0)

    fill(cols, space_pos * col_block, col_block)
    fill(rows, time_pos * row_block, row_block)

    cols[targets, later - snaps :] = jnp.zeros((target_block, snaps), jnp.bfloat16)

    def place_target(piece, block, within):
        @pl.when(block >= 2)
        def _():
            cols[targets, later_at(block - 1, within)] = piece[wanted, :]

        @pl.when(block == 1)
        def _():
            opening_target[:, pl.ds(within, quarter)] = piece[wanted, :]

        @pl.when(block == 0)
        def _():
            opening[:, pl.ds(within, quarter)] = piece[...]

    each_piece(place_target)

    def times(left, right):
        return lax.dot_general(
            left, right, (((1,), (1,)), ((), ())), preferred_element_type=jnp.float32
        ) * (1.0 / (n_time * snaps))

    writes = []
    for step in range(row_block // tile):
        top = step * tile
        at = pl.ds(top, tile)
        product = times(
            rows[pl.ds(LEAD_MODES + top, tile), :],
            cols[pl.ds(LEAD_MODES, col_block + target_block), :],
        )
        shape = (tile, col_block)
        row = time_pos * row_block + top + lax.broadcasted_iota(jnp.int32, shape, 0)
        column = space_pos * col_block + lax.broadcasted_iota(jnp.int32, shape, 1)
        staged[at, :] = product[:, 0:col_block] + jnp.where(row == column, RIDGE_WEIGHT, 0.0)
        side[at, :] = product[:, col_block:]
        if step == 0:

            @pl.when(time_pos == 0)
            def _():
                side[0:modes, :] += times(opening[...], opening_target[...])

            @pl.when((time_pos == 0) & (space_pos == 0))
            def _():
                staged[0:modes, 0:modes] += times(opening[...], opening[...])

        writes.append(pltpu.make_async_copy(staged.at[at], gram_hbm.at[at], sems.at[step]))
        writes[-1].start()
    rhs_ref[...] = side[...].T
    for write in writes:
        write.wait()


def gram_blocks(pieces, n_time, n_space):
    _, modes, quarter = pieces[0].shape
    snaps = QUAD * quarter
    features = modes + 2 * LEAD_MODES * LEAD_MODES
    row_block, col_block, target_block = features // n_time, features // n_space, modes // n_space
    later = (n_time - 1) * snaps
    tile = row_block // 2 if row_block % (2 * ROW_TILE) == 0 else row_block
    assert min(tile, col_block) >= modes
    vmem = pl.BlockSpec(memory_space=pltpu.VMEM)
    gram, rhs = pl.pallas_call(
        functools.partial(
            gram_kernel, (n_time, snaps, modes, row_block, col_block, target_block, tile)
        ),
        out_shape=(
            jax.ShapeDtypeStruct((row_block, col_block), jnp.float32),
            jax.ShapeDtypeStruct((target_block, row_block), jnp.float32),
        ),
        in_specs=[vmem] * len(pieces),
        out_specs=(pl.BlockSpec(memory_space=pl.ANY), vmem),
        scratch_shapes=[
            pltpu.VMEM((2, LEAD_MODES, later), jnp.bfloat16),
            pltpu.VMEM((LEAD_MODES, later), jnp.float32),
            pltpu.VMEM((row_block + 2 * LEAD_MODES, later), jnp.bfloat16),
            pltpu.VMEM((col_block + 2 * LEAD_MODES + target_block, later), jnp.bfloat16),
            pltpu.VMEM((modes, snaps), jnp.bfloat16),
            pltpu.VMEM((target_block, snaps), jnp.bfloat16),
            pltpu.VMEM((row_block, col_block), jnp.float32),
            pltpu.VMEM((row_block, target_block), jnp.float32),
            pltpu.SemaphoreType.DMA((row_block // tile,)),
        ],
        compiler_params=pltpu.CompilerParams(vmem_limit_bytes=VMEM_LIMIT),
        cost_estimate=pl.CostEstimate(
            flops=2 * row_block * (col_block + target_block) * later,
            bytes_accessed=4 * row_block * (col_block + target_block),
            transcendentals=0,
        ),
    )(*map(in_vmem, pieces))
    return gram, rhs.T


def joined(value, axis, bit):
    return jnp.concatenate([value, swap(value, axis, bit)], axis=0)


def per_device(snapshots, modes):
    n_space, n_time = lax.axis_size("space"), lax.axis_size("tm")
    mine, sent = project(modes, snapshots)
    arrived = [swap(part, "space", j) for j, part in enumerate(sent, 1)]
    for part in arrived:
        mine = mine + restored(part)
    for bit in bits_of(n_space)[2:]:
        out = rounded(mine)
        mine = restored(out) + restored(swap(out, "space", bit))
    mine = mine.astype(jnp.bfloat16)[None]
    for bit in bits_of(n_time)[1:]:
        mine = joined(mine, "tm", bit)
    pieces = [mine] + [swap(mine, "space", j) for j in range(1, QUAD)]
    pieces = pieces + [swap(piece, "tm", 1) for piece in pieces]
    return gram_blocks(pieces, n_time, n_space)


def solution(mesh):
    in_specs = (P("space", "tm"), P("space", None))
    out_specs = (P("tm", "space"), P("tm", "space"))
    return jax.shard_map(
        per_device, mesh=mesh, in_specs=in_specs, out_specs=out_specs, check_vma=False
    )
```

```python
import functools

import jax
import jax.numpy as jnp
from jax import lax
from jax.experimental import pallas as pl
from jax.experimental.pallas import tpu as pltpu
from jax.sharding import PartitionSpec as P

LEAD_MODES = 48
RIDGE_WEIGHT = 0.05
ROW_TILE = 16
QUAD = 4
PROJECTION_STEPS = 10
VMEM_LIMIT = 48 * 2**20


def swap(value, axis, bit):
    count = lax.axis_size(axis)
    return lax.ppermute(value, axis, [(i, i ^ bit) for i in range(count)])


def bits_of(count):
    return [1 << k for k in range(count.bit_length() - 1)]


def in_hbm(value):
    return pltpu.with_memory_space_constraint(value, pltpu.HBM)


def in_vmem(value):
    return pltpu.with_memory_space_constraint(value, pltpu.VMEM)


def rounded(value):
    high = lax.reduce_precision(value, 8, 7)
    left = value[0:LEAD_MODES] - high[0:LEAD_MODES]
    return jnp.concatenate([high, left], axis=0).astype(jnp.bfloat16)


def restored(value):
    modes = value.shape[0] - LEAD_MODES
    whole = value[0:modes].astype(jnp.float32)
    left = value[modes:].astype(jnp.float32)
    return jnp.concatenate([whole[0:LEAD_MODES] + left, whole[LEAD_MODES:]], axis=0)


def projection_kernel(modes_hbm, snaps_hbm, own_ref, *refs):
    sent_refs, (modes, snaps, partial_sums, modes_sems, snaps_sems) = refs[0:3], refs[3:]
    depth = modes.shape[0] // PROJECTION_STEPS
    quarter = snaps.shape[1] // QUAD

    def copies(step):
        at = pl.ds(step * depth, depth)
        return (
            pltpu.make_async_copy(modes_hbm.at[at], modes.at[at], modes_sems.at[step]),
            pltpu.make_async_copy(snaps_hbm.at[at], snaps.at[at], snaps_sems.at[step]),
        )

    for step in range(PROJECTION_STEPS):
        for copy in copies(step):
            copy.start()
    for step in range(PROJECTION_STEPS):
        for copy in copies(step):
            copy.wait()
        at = pl.ds(step * depth, depth)
        product = lax.dot_general(
            modes[at, :],
            snaps[at, :],
            (((0,), (0,)), ((), ())),
            preferred_element_type=jnp.float32,
        )
        if step == 0:
            partial_sums[...] = product
        else:
            partial_sums[...] += product
    place = lax.rem(lax.axis_index("space"), QUAD)
    count = partial_sums.shape[0]
    for j in range(QUAD):
        start = pl.multiple_of(jnp.bitwise_xor(place, j) * quarter, quarter)
        part = partial_sums[:, pl.ds(start, quarter)]
        if j == 0:
            own_ref[...] = part
        else:
            high = part.astype(jnp.bfloat16)
            left = part[0:LEAD_MODES] - high[0:LEAD_MODES].astype(jnp.float32)
            sent_refs[j - 1][0:count, :] = high
            sent_refs[j - 1][count:, :] = left.astype(jnp.bfloat16)


def project(modes, snapshots):
    (depth, count), snaps = modes.shape, snapshots.shape[1]
    quarter = snaps // QUAD
    vmem = pl.BlockSpec(memory_space=pltpu.VMEM)
    anywhere = pl.BlockSpec(memory_space=pltpu.HBM)
    own, *sent = pl.pallas_call(
        projection_kernel,
        out_shape=(pltpu.VMEM((count, quarter), jnp.float32),)
        + (pltpu.VMEM((count + LEAD_MODES, quarter), jnp.bfloat16),) * (QUAD - 1),
        in_specs=[anywhere] * 2,
        out_specs=(vmem,) * QUAD,
        scratch_shapes=[
            pltpu.VMEM((depth, count), jnp.bfloat16),
            pltpu.VMEM((depth, snaps), jnp.bfloat16),
            pltpu.VMEM((count, snaps), jnp.float32),
            pltpu.SemaphoreType.DMA((PROJECTION_STEPS,)),
            pltpu.SemaphoreType.DMA((PROJECTION_STEPS,)),
        ],
        compiler_params=pltpu.CompilerParams(vmem_limit_bytes=VMEM_LIMIT),
        cost_estimate=pl.CostEstimate(
            flops=2 * depth * count * snaps,
            bytes_accessed=2 * depth * (count + snaps),
            transcendentals=0,
        ),
    )(in_hbm(modes), in_hbm(snapshots))
    return own, sent


def gram_kernel(sizes, *refs):
    n_time, snaps, modes, row_block, col_block, target_block, tops = sizes
    half, quarter = n_time // 2, snaps // QUAD
    count = 2 * QUAD
    pieces, (gram_hbm, rhs_ref) = refs[0:count], refs[count : count + 2]
    lead, head, target, coeffs, rows, cols, staged, side, sems = refs[count + 2 :]
    later = (n_time - 1) * snaps
    time_pos, space_pos = lax.axis_index("tm"), lax.axis_index("space")
    place = lax.rem(space_pos, QUAD)

    def each_piece(take):
        for other in range(2):
            for k in range(half):
                block = jnp.bitwise_xor(time_pos, 2 * k + other)
                for j in range(QUAD):
                    at = block * snaps + jnp.bitwise_xor(place, j) * quarter
                    take(pieces[other * QUAD + j].at[k], pl.multiple_of(at, quarter))

    gap = 2 * snaps
    lead[:, 0:gap] = jnp.zeros((LEAD_MODES, gap), jnp.bfloat16)
    target[:, n_time * snaps :] = jnp.zeros((target_block, snaps), jnp.bfloat16)
    wanted = pl.ds(pl.multiple_of(space_pos * target_block, ROW_TILE), target_block)

    def place_lead(piece, at):
        current = piece[0:LEAD_MODES, :]
        head[:, pl.ds(at, quarter)] = current.astype(jnp.float32)
        lead[:, pl.ds(at + gap, quarter)] = current
        target[:, pl.ds(at, quarter)] = piece[wanted, :]

    each_piece(place_lead)

    @pl.when((time_pos == 0) | (space_pos == 0))
    def _():
        def place_modes(piece, at):
            coeffs[:, pl.ds(at, quarter)] = piece[...]

        each_piece(place_modes)

    def fill(out, start, extent):
        @pl.when(start == 0)
        def _():
            out[pl.ds(LEAD_MODES, modes), :] = coeffs[:, snaps:]

        def group(q, carry):
            kind, i = lax.div(q, LEAD_MODES), lax.rem(q, LEAD_MODES)
            at = modes + LEAD_MODES * q - start + LEAD_MODES
            factor = jnp.broadcast_to(head[pl.ds(i, 1), snaps:], (ROW_TILE, later)).astype(
                jnp.bfloat16
            )
            shifted = pl.ds(pl.multiple_of(gap - kind * snaps, snaps), later)
            for j in range(0, LEAD_MODES, ROW_TILE):
                out[pl.ds(pl.multiple_of(at + j, ROW_TILE), ROW_TILE), :] = (
                    factor * lead[j : j + ROW_TILE, shifted]
                )
            return carry

        first = jnp.maximum(0, lax.div(start - modes, LEAD_MODES))
        last = lax.div(start + extent - modes + LEAD_MODES - 1, LEAD_MODES)
        lax.fori_loop(first, last, group, 0)

    fill(cols, space_pos * col_block, col_block)
    fill(rows, time_pos * row_block, row_block)
    cols[pl.ds(LEAD_MODES + col_block, target_block), :] = target[:, gap:]

    def times(left, right):
        return lax.dot_general(
            left, right, (((1,), (1,)), ((), ())), preferred_element_type=jnp.float32
        ) * (1.0 / (n_time * snaps))

    writes = []
    for step, top in enumerate(tops):
        tile = (tops + (row_block,))[step + 1] - top
        at = pl.ds(top, tile)
        product = times(
            rows[pl.ds(LEAD_MODES + top, tile), :],
            cols[pl.ds(LEAD_MODES, col_block + target_block), :],
        )
        shape = (tile, col_block)
        row = time_pos * row_block + top + lax.broadcasted_iota(jnp.int32, shape, 0)
        column = space_pos * col_block + lax.broadcasted_iota(jnp.int32, shape, 1)
        staged[at, :] = product[:, 0:col_block] + jnp.where(row == column, RIDGE_WEIGHT, 0.0)
        side[at, :] = product[:, col_block:]
        if step == 0:

            @pl.when(time_pos == 0)
            def _():
                side[0:modes, :] += times(coeffs[:, 0:snaps], target[:, snaps:gap])

            @pl.when((time_pos == 0) & (space_pos == 0))
            def _():
                staged[0:modes, 0:modes] += times(coeffs[:, 0:snaps], coeffs[:, 0:snaps])

        writes.append(pltpu.make_async_copy(staged.at[at], gram_hbm.at[at], sems.at[step]))
        writes[-1].start()
    rhs_ref[...] = side[...].T
    for write in writes:
        write.wait()


def gram_blocks(pieces, n_time, n_space):
    _, modes, quarter = pieces[0].shape
    snaps = QUAD * quarter
    features = modes + 2 * LEAD_MODES * LEAD_MODES
    row_block, col_block, target_block = features // n_time, features // n_space, modes // n_space
    later = (n_time - 1) * snaps
    last = row_block // ROW_TILE // 4 * ROW_TILE
    tops = (0, row_block - last) if row_block - last >= modes else (0,)
    assert min(row_block, col_block) >= modes
    vmem = pl.BlockSpec(memory_space=pltpu.VMEM)
    gram, rhs = pl.pallas_call(
        functools.partial(
            gram_kernel, (n_time, snaps, modes, row_block, col_block, target_block, tops)
        ),
        out_shape=(
            jax.ShapeDtypeStruct((row_block, col_block), jnp.float32),
            jax.ShapeDtypeStruct((target_block, row_block), jnp.float32),
        ),
        in_specs=[vmem] * len(pieces),
        out_specs=(pl.BlockSpec(memory_space=pl.ANY), vmem),
        scratch_shapes=[
            pltpu.VMEM((LEAD_MODES, (n_time + 2) * snaps), jnp.bfloat16),
            pltpu.VMEM((LEAD_MODES, n_time * snaps), jnp.float32),
            pltpu.VMEM((target_block, (n_time + 1) * snaps), jnp.bfloat16),
            pltpu.VMEM((modes, n_time * snaps), jnp.bfloat16),
            pltpu.VMEM((row_block + 2 * LEAD_MODES, later), jnp.bfloat16),
            pltpu.VMEM((col_block + 2 * LEAD_MODES + target_block, later), jnp.bfloat16),
            pltpu.VMEM((row_block, col_block), jnp.float32),
            pltpu.VMEM((row_block, target_block), jnp.float32),
            pltpu.SemaphoreType.DMA((len(tops),)),
        ],
        compiler_params=pltpu.CompilerParams(vmem_limit_bytes=VMEM_LIMIT),
        cost_estimate=pl.CostEstimate(
            flops=2 * row_block * (col_block + target_block) * later,
            bytes_accessed=4 * row_block * (col_block + target_block),
            transcendentals=0,
        ),
    )(*map(in_vmem, pieces))
    return gram, rhs.T


def joined(value, axis, bit):
    return jnp.concatenate([value, swap(value, axis, bit)], axis=0)


def per_device(snapshots, modes):
    n_space, n_time = lax.axis_size("space"), lax.axis_size("tm")
    mine, sent = project(modes, snapshots)
    arrived = [swap(part, "space", j) for j, part in enumerate(sent, 1)]
    for part in arrived:
        mine = mine + restored(part)
    for bit in bits_of(n_space)[2:]:
        out = rounded(mine)
        mine = restored(out) + restored(swap(out, "space", bit))
    mine = mine.astype(jnp.bfloat16)[None]
    for bit in bits_of(n_time)[1:]:
        mine = joined(mine, "tm", bit)
    pieces = [mine] + [swap(mine, "space", j) for j in range(1, QUAD)]
    pieces = pieces + [swap(piece, "tm", 1) for piece in pieces]
    return gram_blocks(pieces, n_time, n_space)


def solution(mesh):
    in_specs = (P("space", "tm"), P("space", None))
    out_specs = (P("tm", "space"), P("tm", "space"))
    return jax.shard_map(
        per_device, mesh=mesh, in_specs=in_specs, out_specs=out_specs, check_vma=False
    )
```

```python
import functools

import jax
import jax.numpy as jnp
from jax import lax
from jax.experimental import pallas as pl
from jax.experimental.pallas import tpu as pltpu
from jax.sharding import PartitionSpec as P

LEAD_MODES = 48
RIDGE_WEIGHT = 0.05
ROW_TILE = 16
QUAD = 4
PROJECTION_STEPS = 10
VMEM_LIMIT = 48 * 2**20


def swap(value, axis, bit):
    count = lax.axis_size(axis)
    return lax.ppermute(value, axis, [(i, i ^ bit) for i in range(count)])


def bits_of(count):
    return [1 << k for k in range(count.bit_length() - 1)]


def in_hbm(value):
    return pltpu.with_memory_space_constraint(value, pltpu.HBM)


def in_vmem(value):
    return pltpu.with_memory_space_constraint(value, pltpu.VMEM)


def rounded(value):
    high = lax.reduce_precision(value, 8, 7)
    left = value[0:LEAD_MODES] - high[0:LEAD_MODES]
    return jnp.concatenate([high, left], axis=0).astype(jnp.bfloat16)


def restored(value):
    modes = value.shape[0] - LEAD_MODES
    whole = value[0:modes].astype(jnp.float32)
    left = value[modes:].astype(jnp.float32)
    return jnp.concatenate([whole[0:LEAD_MODES] + left, whole[LEAD_MODES:]], axis=0)


def projection_kernel(modes_hbm, snaps_hbm, own_ref, *refs):
    sent_refs, (modes, snaps, partial_sums, modes_sems, snaps_sems) = refs[0:3], refs[3:]
    depth = modes.shape[0] // PROJECTION_STEPS
    quarter = snaps.shape[1] // QUAD

    def copies(step):
        at = pl.ds(step * depth, depth)
        return (
            pltpu.make_async_copy(modes_hbm.at[at], modes.at[at], modes_sems.at[step]),
            pltpu.make_async_copy(snaps_hbm.at[at], snaps.at[at], snaps_sems.at[step]),
        )

    for step in range(PROJECTION_STEPS):
        for copy in copies(step):
            copy.start()
    for step in range(PROJECTION_STEPS):
        for copy in copies(step):
            copy.wait()
        at = pl.ds(step * depth, depth)
        product = lax.dot_general(
            modes[at, :],
            snaps[at, :],
            (((0,), (0,)), ((), ())),
            preferred_element_type=jnp.float32,
        )
        if step == 0:
            partial_sums[...] = product
        else:
            partial_sums[...] += product
    place = lax.rem(lax.axis_index("space"), QUAD)
    count = partial_sums.shape[0]
    for j in range(QUAD):
        start = pl.multiple_of(jnp.bitwise_xor(place, j) * quarter, quarter)
        part = partial_sums[:, pl.ds(start, quarter)]
        if j == 0:
            own_ref[...] = part
        else:
            high = part.astype(jnp.bfloat16)
            left = part[0:LEAD_MODES] - high[0:LEAD_MODES].astype(jnp.float32)
            sent_refs[j - 1][0:count, :] = high
            sent_refs[j - 1][count:, :] = left.astype(jnp.bfloat16)


def project(modes, snapshots):
    (depth, count), snaps = modes.shape, snapshots.shape[1]
    quarter = snaps // QUAD
    vmem = pl.BlockSpec(memory_space=pltpu.VMEM)
    anywhere = pl.BlockSpec(memory_space=pltpu.HBM)
    own, *sent = pl.pallas_call(
        projection_kernel,
        out_shape=(pltpu.VMEM((count, quarter), jnp.float32),)
        + (pltpu.VMEM((count + LEAD_MODES, quarter), jnp.bfloat16),) * (QUAD - 1),
        in_specs=[anywhere] * 2,
        out_specs=(vmem,) * QUAD,
        scratch_shapes=[
            pltpu.VMEM((depth, count), jnp.bfloat16),
            pltpu.VMEM((depth, snaps), jnp.bfloat16),
            pltpu.VMEM((count, snaps), jnp.float32),
            pltpu.SemaphoreType.DMA((PROJECTION_STEPS,)),
            pltpu.SemaphoreType.DMA((PROJECTION_STEPS,)),
        ],
        compiler_params=pltpu.CompilerParams(vmem_limit_bytes=VMEM_LIMIT),
        cost_estimate=pl.CostEstimate(
            flops=2 * depth * count * snaps,
            bytes_accessed=2 * depth * (count + snaps),
            transcendentals=0,
        ),
    )(in_hbm(modes), in_hbm(snapshots))
    return own, sent


def gram_kernel(sizes, *refs):
    n_time, snaps, modes, row_block, col_block, target_block, tile = sizes
    half, quarter = n_time // 2, snaps // QUAD
    count = 2 * QUAD
    pieces, (gram_hbm, rhs_ref) = refs[0:count], refs[count : count + 2]
    lead, head, target, coeffs, *rows, cols, staged, side, sems = refs[count + 2 :]
    later = (n_time - 1) * snaps
    time_pos, space_pos = lax.axis_index("tm"), lax.axis_index("space")
    place = lax.rem(space_pos, QUAD)

    def each_piece(take):
        for other in range(2):
            for k in range(half):
                block = jnp.bitwise_xor(time_pos, 2 * k + other)
                for j in range(QUAD):
                    at = block * snaps + jnp.bitwise_xor(place, j) * quarter
                    take(pieces[other * QUAD + j].at[k], pl.multiple_of(at, quarter))

    gap = 2 * snaps
    lead[:, 0:gap] = jnp.zeros((LEAD_MODES, gap), jnp.bfloat16)
    target[:, n_time * snaps :] = jnp.zeros((target_block, snaps), jnp.bfloat16)
    wanted = pl.ds(pl.multiple_of(space_pos * target_block, ROW_TILE), target_block)

    def place_lead(piece, at):
        current = piece[0:LEAD_MODES, :]
        head[:, pl.ds(at, quarter)] = current.astype(jnp.float32)
        lead[:, pl.ds(at + gap, quarter)] = current
        target[:, pl.ds(at, quarter)] = piece[wanted, :]

    each_piece(place_lead)

    @pl.when((time_pos == 0) | (space_pos == 0))
    def _():
        def place_modes(piece, at):
            coeffs[:, pl.ds(at, quarter)] = piece[...]

        each_piece(place_modes)

    def build_group(out, q, at):
        kind, i = lax.div(q, LEAD_MODES), lax.rem(q, LEAD_MODES)
        factor = jnp.broadcast_to(head[pl.ds(i, 1), snaps:], (ROW_TILE, later)).astype(
            jnp.bfloat16
        )
        shifted = pl.ds(pl.multiple_of(gap - kind * snaps, snaps), later)
        for j in range(0, LEAD_MODES, ROW_TILE):
            out[pl.ds(pl.multiple_of(at + j, ROW_TILE), ROW_TILE), :] = (
                factor * lead[j : j + ROW_TILE, shifted]
            )

    def fill(out, start, extent):
        @pl.when(start == 0)
        def _():
            out[pl.ds(LEAD_MODES, modes), :] = coeffs[:, snaps:]

        def group(q, carry):
            build_group(out, q, modes + LEAD_MODES * q - start + LEAD_MODES)
            return carry

        first = jnp.maximum(0, lax.div(start - modes, LEAD_MODES))
        last = lax.div(start + extent - modes + LEAD_MODES - 1, LEAD_MODES)
        lax.fori_loop(first, last, group, 0)

    def fill_products(out, start, extent):
        first = lax.div(start - modes, LEAD_MODES)
        most = 2 * LEAD_MODES - 1
        for g in range(-(-(extent + LEAD_MODES - ROW_TILE) // LEAD_MODES)):
            at = modes + LEAD_MODES * (first + g) - start + LEAD_MODES
            build_group(out, jnp.minimum(first + g, most), at)

    row_start = time_pos * row_block
    fill(cols, space_pos * col_block, col_block)
    fill(rows[0], row_start, tile)
    cols[pl.ds(LEAD_MODES + col_block, target_block), :] = target[:, gap:]

    def times(left, right):
        return lax.dot_general(
            left, right, (((1,), (1,)), ((), ())), preferred_element_type=jnp.float32
        ) * (1.0 / (n_time * snaps))

    writes = []
    for step in range(row_block // tile):
        top = step * tile
        at = pl.ds(top, tile)
        if top + tile < row_block:
            fill_products(rows[(step + 1) % 2], row_start + top + tile, tile)
        product = times(
            rows[step % 2][pl.ds(LEAD_MODES, tile), :],
            cols[pl.ds(LEAD_MODES, col_block + target_block), :],
        )
        shape = (tile, col_block)
        row = time_pos * row_block + top + lax.broadcasted_iota(jnp.int32, shape, 0)
        column = space_pos * col_block + lax.broadcasted_iota(jnp.int32, shape, 1)
        staged[at, :] = product[:, 0:col_block] + jnp.where(row == column, RIDGE_WEIGHT, 0.0)
        side[at, :] = product[:, col_block:]
        if step == 0:

            @pl.when(time_pos == 0)
            def _():
                side[0:modes, :] += times(coeffs[:, 0:snaps], target[:, snaps:gap])

            @pl.when((time_pos == 0) & (space_pos == 0))
            def _():
                staged[0:modes, 0:modes] += times(coeffs[:, 0:snaps], coeffs[:, 0:snaps])

        writes.append(pltpu.make_async_copy(staged.at[at], gram_hbm.at[at], sems.at[step]))
        writes[-1].start()
    rhs_ref[...] = side[...].T
    for write in writes:
        write.wait()


def gram_blocks(pieces, n_time, n_space):
    _, modes, quarter = pieces[0].shape
    snaps = QUAD * quarter
    features = modes + 2 * LEAD_MODES * LEAD_MODES
    row_block, col_block, target_block = features // n_time, features // n_space, modes // n_space
    later = (n_time - 1) * snaps
    tile = row_block // 4 if row_block % (4 * ROW_TILE) == 0 else row_block
    assert min(tile, col_block) >= modes
    vmem = pl.BlockSpec(memory_space=pltpu.VMEM)
    gram, rhs = pl.pallas_call(
        functools.partial(
            gram_kernel, (n_time, snaps, modes, row_block, col_block, target_block, tile)
        ),
        out_shape=(
            jax.ShapeDtypeStruct((row_block, col_block), jnp.float32),
            jax.ShapeDtypeStruct((target_block, row_block), jnp.float32),
        ),
        in_specs=[vmem] * len(pieces),
        out_specs=(pl.BlockSpec(memory_space=pl.ANY), vmem),
        scratch_shapes=[
            pltpu.VMEM((LEAD_MODES, (n_time + 2) * snaps), jnp.bfloat16),
            pltpu.VMEM((LEAD_MODES, n_time * snaps), jnp.float32),
            pltpu.VMEM((target_block, (n_time + 1) * snaps), jnp.bfloat16),
            pltpu.VMEM((modes, n_time * snaps), jnp.bfloat16),
            pltpu.VMEM((tile + 2 * LEAD_MODES, later), jnp.bfloat16),
            pltpu.VMEM((tile + 2 * LEAD_MODES, later), jnp.bfloat16),
            pltpu.VMEM((col_block + 2 * LEAD_MODES + target_block, later), jnp.bfloat16),
            pltpu.VMEM((row_block, col_block), jnp.float32),
            pltpu.VMEM((row_block, target_block), jnp.float32),
            pltpu.SemaphoreType.DMA((row_block // tile,)),
        ],
        compiler_params=pltpu.CompilerParams(vmem_limit_bytes=VMEM_LIMIT),
        cost_estimate=pl.CostEstimate(
            flops=2 * row_block * (col_block + target_block) * later,
            bytes_accessed=4 * row_block * (col_block + target_block),
            transcendentals=0,
        ),
    )(*map(in_vmem, pieces))
    return gram, rhs.T


def joined(value, axis, bit):
    return jnp.concatenate([value, swap(value, axis, bit)], axis=0)


def per_device(snapshots, modes):
    n_space, n_time = lax.axis_size("space"), lax.axis_size("tm")
    mine, sent = project(modes, snapshots)
    arrived = [swap(part, "space", j) for j, part in enumerate(sent, 1)]
    for part in arrived:
        mine = mine + restored(part)
    for bit in bits_of(n_space)[2:]:
        out = rounded(mine)
        mine = restored(out) + restored(swap(out, "space", bit))
    mine = mine.astype(jnp.bfloat16)[None]
    for bit in bits_of(n_time)[1:]:
        mine = joined(mine, "tm", bit)
    pieces = [mine] + [swap(mine, "space", j) for j in range(1, QUAD)]
    pieces = pieces + [swap(piece, "tm", 1) for piece in pieces]
    return gram_blocks(pieces, n_time, n_space)


def solution(mesh):
    in_specs = (P("space", "tm"), P("space", None))
    out_specs = (P("tm", "space"), P("tm", "space"))
    return jax.shard_map(
        per_device, mesh=mesh, in_specs=in_specs, out_specs=out_specs, check_vma=False
    )
```

```python
import functools

import jax
import jax.numpy as jnp
from jax import lax
from jax.experimental import pallas as pl
from jax.experimental.pallas import tpu as pltpu
from jax.sharding import PartitionSpec as P

LEAD_MODES = 48
RIDGE_WEIGHT = 0.05
ROW_TILE = 16
QUAD = 4
PROJECTION_STEPS = 10
VMEM_LIMIT = 48 * 2**20


def swap(value, axis, bit):
    count = lax.axis_size(axis)
    return lax.ppermute(value, axis, [(i, i ^ bit) for i in range(count)])


def bits_of(count):
    return [1 << k for k in range(count.bit_length() - 1)]


def in_hbm(value):
    return pltpu.with_memory_space_constraint(value, pltpu.HBM)


def in_vmem(value):
    return pltpu.with_memory_space_constraint(value, pltpu.VMEM)


def rounded(value):
    high = lax.reduce_precision(value, 8, 7)
    left = value[0:LEAD_MODES] - high[0:LEAD_MODES]
    return jnp.concatenate([high, left], axis=0).astype(jnp.bfloat16)


def restored(value):
    modes = value.shape[0] - LEAD_MODES
    whole = value[0:modes].astype(jnp.float32)
    left = value[modes:].astype(jnp.float32)
    return jnp.concatenate([whole[0:LEAD_MODES] + left, whole[LEAD_MODES:]], axis=0)


def projection_kernel(modes_hbm, snaps_hbm, own_ref, *refs):
    sent_refs, (modes, snaps, partial_sums, modes_sems, snaps_sems) = refs[0:3], refs[3:]
    depth = modes.shape[0] // PROJECTION_STEPS
    quarter = snaps.shape[1] // QUAD

    def copies(step):
        at = pl.ds(step * depth, depth)
        return (
            pltpu.make_async_copy(modes_hbm.at[at], modes.at[at], modes_sems.at[step]),
            pltpu.make_async_copy(snaps_hbm.at[at], snaps.at[at], snaps_sems.at[step]),
        )

    for step in range(PROJECTION_STEPS):
        for copy in copies(step):
            copy.start()
    for step in range(PROJECTION_STEPS):
        for copy in copies(step):
            copy.wait()
        at = pl.ds(step * depth, depth)
        product = lax.dot_general(
            modes[at, :],
            snaps[at, :],
            (((0,), (0,)), ((), ())),
            preferred_element_type=jnp.float32,
        )
        if step == 0:
            partial_sums[...] = product
        else:
            partial_sums[...] += product
    place = lax.rem(lax.axis_index("space"), QUAD)
    count = partial_sums.shape[0]
    for j in range(QUAD):
        start = pl.multiple_of(jnp.bitwise_xor(place, j) * quarter, quarter)
        part = partial_sums[:, pl.ds(start, quarter)]
        if j == 0:
            own_ref[...] = part
        else:
            high = part.astype(jnp.bfloat16)
            left = part[0:LEAD_MODES] - high[0:LEAD_MODES].astype(jnp.float32)
            sent_refs[j - 1][0:count, :] = high
            sent_refs[j - 1][count:, :] = left.astype(jnp.bfloat16)


def project(modes, snapshots):
    (depth, count), snaps = modes.shape, snapshots.shape[1]
    quarter = snaps // QUAD
    vmem = pl.BlockSpec(memory_space=pltpu.VMEM)
    anywhere = pl.BlockSpec(memory_space=pltpu.HBM)
    own, *sent = pl.pallas_call(
        projection_kernel,
        out_shape=(pltpu.VMEM((count, quarter), jnp.float32),)
        + (pltpu.VMEM((count + LEAD_MODES, quarter), jnp.bfloat16),) * (QUAD - 1),
        in_specs=[anywhere] * 2,
        out_specs=(vmem,) * QUAD,
        scratch_shapes=[
            pltpu.VMEM((depth, count), jnp.bfloat16),
            pltpu.VMEM((depth, snaps), jnp.bfloat16),
            pltpu.VMEM((count, snaps), jnp.float32),
            pltpu.SemaphoreType.DMA((PROJECTION_STEPS,)),
            pltpu.SemaphoreType.DMA((PROJECTION_STEPS,)),
        ],
        compiler_params=pltpu.CompilerParams(vmem_limit_bytes=VMEM_LIMIT),
        cost_estimate=pl.CostEstimate(
            flops=2 * depth * count * snaps,
            bytes_accessed=2 * depth * (count + snaps),
            transcendentals=0,
        ),
    )(in_hbm(modes), in_hbm(snapshots))
    return own, sent


def gram_kernel(sizes, *refs):
    n_time, snaps, modes, row_block, col_block, target_block, tile = sizes
    half, quarter = n_time // 2, snaps // QUAD
    count = 2 * QUAD
    pieces, (gram_hbm, rhs_hbm) = refs[0:count], refs[count : count + 2]
    lead, head, target, *rows, cols, staged, side, side_staged, sems = refs[count + 2 :]
    later = (n_time - 1) * snaps
    time_pos, space_pos = lax.axis_index("tm"), lax.axis_index("space")
    place = lax.rem(space_pos, QUAD)

    def each_piece(take):
        for other in range(2):
            for k in range(half):
                block = jnp.bitwise_xor(time_pos, 2 * k + other)
                for j in range(QUAD):
                    at = block * snaps + jnp.bitwise_xor(place, j) * quarter
                    take(pieces[other * QUAD + j].at[k], pl.multiple_of(at, quarter))

    gap = 2 * snaps
    lead[:, 0:gap] = jnp.zeros((LEAD_MODES, gap), jnp.bfloat16)
    target[:, n_time * snaps :] = jnp.zeros((target_block, snaps), jnp.bfloat16)
    wanted = pl.ds(pl.multiple_of(space_pos * target_block, ROW_TILE), target_block)

    def place_lead(piece, at):
        current = piece[0:LEAD_MODES, :]
        head[:, pl.ds(at, quarter)] = current.astype(jnp.float32)
        lead[:, pl.ds(at + gap, quarter)] = current
        target[:, pl.ds(at, quarter)] = piece[wanted, :]

    each_piece(place_lead)

    def build_group(out, q, at):
        kind, i = lax.div(q, LEAD_MODES), lax.rem(q, LEAD_MODES)
        factor = jnp.broadcast_to(head[pl.ds(i, 1), snaps:], (ROW_TILE, later)).astype(
            jnp.bfloat16
        )
        shifted = pl.ds(pl.multiple_of(gap - kind * snaps, snaps), later)
        for j in range(0, LEAD_MODES, ROW_TILE):
            out[pl.ds(pl.multiple_of(at + j, ROW_TILE), ROW_TILE), snaps:] = (
                factor * lead[j : j + ROW_TILE, shifted]
            )

    def fill(out, start, extent):
        @pl.when(start == 0)
        def _():
            def place_modes(piece, at):
                out[pl.ds(LEAD_MODES, modes), pl.ds(at, quarter)] = piece[...]

            each_piece(place_modes)

        def group(q, carry):
            build_group(out, q, modes + LEAD_MODES * q - start + LEAD_MODES)
            return carry

        first = jnp.maximum(0, lax.div(start - modes, LEAD_MODES))
        last = lax.div(start + extent - modes + LEAD_MODES - 1, LEAD_MODES)
        lax.fori_loop(first, last, group, 0)

    def fill_products(out, start, extent):
        first = lax.div(start - modes, LEAD_MODES)
        most = 2 * LEAD_MODES - 1
        for g in range(-(-(extent + LEAD_MODES - ROW_TILE) // LEAD_MODES)):
            at = modes + LEAD_MODES * (first + g) - start + LEAD_MODES
            build_group(out, jnp.minimum(first + g, most), at)

    row_start = time_pos * row_block
    fill(cols, space_pos * col_block, col_block)
    fill(rows[0], row_start, tile)
    cols[pl.ds(LEAD_MODES + col_block, target_block), snaps:] = target[:, gap:]

    def times(left, right):
        return lax.dot_general(
            left, right, (((1,), (1,)), ((), ())), preferred_element_type=jnp.float32
        ) * (1.0 / (n_time * snaps))

    first_rows = rows[0].at[pl.ds(LEAD_MODES, modes), 0:snaps]
    first_cols = cols.at[pl.ds(LEAD_MODES, modes), 0:snaps]
    writes = []
    for step in range(row_block // tile):
        top = step * tile
        at = pl.ds(top, tile)
        if top + tile < row_block:
            fill_products(rows[(step + 1) % 2], row_start + top + tile, tile)
        product = times(
            rows[step % 2][pl.ds(LEAD_MODES, tile), snaps:],
            cols[pl.ds(LEAD_MODES, col_block + target_block), snaps:],
        )
        shape = (tile, col_block)
        row = time_pos * row_block + top + lax.broadcasted_iota(jnp.int32, shape, 0)
        column = space_pos * col_block + lax.broadcasted_iota(jnp.int32, shape, 1)
        staged[at, :] = product[:, 0:col_block] + jnp.where(row == column, RIDGE_WEIGHT, 0.0)
        side[at, :] = product[:, col_block:]
        if step == 0:

            @pl.when(time_pos == 0)
            def _():
                side[0:modes, :] += times(first_rows[...], target[:, snaps:gap])

            @pl.when((time_pos == 0) & (space_pos == 0))
            def _():
                staged[0:modes, 0:modes] += times(
                    first_rows[...], first_cols[...]
                )

        writes.append(pltpu.make_async_copy(staged.at[at], gram_hbm.at[at], sems.at[step]))
        writes[-1].start()
    side_staged[...] = side[...].T
    writes.append(pltpu.make_async_copy(side_staged, rhs_hbm, sems.at[len(writes)]))
    writes[-1].start()
    for write in writes:
        write.wait()


def gram_blocks(pieces, n_time, n_space):
    _, modes, quarter = pieces[0].shape
    snaps = QUAD * quarter
    features = modes + 2 * LEAD_MODES * LEAD_MODES
    row_block, col_block, target_block = features // n_time, features // n_space, modes // n_space
    later = (n_time - 1) * snaps
    tile = row_block // 4 if row_block % (4 * ROW_TILE) == 0 else row_block
    assert min(tile, col_block) >= modes
    vmem = pl.BlockSpec(memory_space=pltpu.VMEM)
    gram, rhs = pl.pallas_call(
        functools.partial(
            gram_kernel, (n_time, snaps, modes, row_block, col_block, target_block, tile)
        ),
        out_shape=(
            jax.ShapeDtypeStruct((row_block, col_block), jnp.float32),
            jax.ShapeDtypeStruct((target_block, row_block), jnp.float32),
        ),
        in_specs=[vmem] * len(pieces),
        out_specs=(pl.BlockSpec(memory_space=pl.ANY),) * 2,
        scratch_shapes=[
            pltpu.VMEM((LEAD_MODES, (n_time + 2) * snaps), jnp.bfloat16),
            pltpu.VMEM((LEAD_MODES, n_time * snaps), jnp.float32),
            pltpu.VMEM((target_block, (n_time + 1) * snaps), jnp.bfloat16),
            pltpu.VMEM((tile + 2 * LEAD_MODES, n_time * snaps), jnp.bfloat16),
            pltpu.VMEM((tile + 2 * LEAD_MODES, n_time * snaps), jnp.bfloat16),
            pltpu.VMEM((col_block + 2 * LEAD_MODES + target_block, n_time * snaps), jnp.bfloat16),
            pltpu.VMEM((row_block, col_block), jnp.float32),
            pltpu.VMEM((row_block, target_block), jnp.float32),
            pltpu.VMEM((target_block, row_block), jnp.float32),
            pltpu.SemaphoreType.DMA((row_block // tile + 1,)),
        ],
        compiler_params=pltpu.CompilerParams(vmem_limit_bytes=VMEM_LIMIT),
        cost_estimate=pl.CostEstimate(
            flops=2 * row_block * (col_block + target_block) * later,
            bytes_accessed=4 * row_block * (col_block + target_block),
            transcendentals=0,
        ),
    )(*map(in_vmem, pieces))
    return gram, rhs.T


def joined(value, axis, bit):
    return jnp.concatenate([value, swap(value, axis, bit)], axis=0)


def per_device(snapshots, modes):
    n_space, n_time = lax.axis_size("space"), lax.axis_size("tm")
    mine, sent = project(modes, snapshots)
    arrived = [swap(part, "space", j) for j, part in enumerate(sent, 1)]
    for part in arrived:
        mine = mine + restored(part)
    for bit in bits_of(n_space)[2:]:
        out = rounded(mine)
        mine = restored(out) + restored(swap(out, "space", bit))
    mine = mine.astype(jnp.bfloat16)[None]
    for bit in bits_of(n_time)[1:]:
        mine = joined(mine, "tm", bit)
    pieces = [mine] + [swap(mine, "space", j) for j in range(1, QUAD)]
    pieces = pieces + [swap(piece, "tm", 1) for piece in pieces]
    return gram_blocks(pieces, n_time, n_space)


def solution(mesh):
    in_specs = (P("space", "tm"), P("space", None))
    out_specs = (P("tm", "space"), P("tm", "space"))
    return jax.shard_map(
        per_device, mesh=mesh, in_specs=in_specs, out_specs=out_specs, check_vma=False
    )
```

```python
import functools

import jax
import jax.numpy as jnp
from jax import lax
from jax.experimental import pallas as pl
from jax.experimental.pallas import tpu as pltpu
from jax.sharding import PartitionSpec as P

LEAD_MODES = 48
RIDGE_WEIGHT = 0.05
ROW_TILE = 16
QUAD = 4
PROJECTION_STEPS = 10
EXPONENT_ROWS = 8
TOP = 9.0
SMALLEST = 1e-30
VMEM_LIMIT = 48 * 2**20


def swap(value, axis, bit):
    count = lax.axis_size(axis)
    return lax.ppermute(value, axis, [(i, i ^ bit) for i in range(count)])


def bits_of(count):
    return [1 << k for k in range(count.bit_length() - 1)]


def in_hbm(value):
    return pltpu.with_memory_space_constraint(value, pltpu.HBM)


def in_vmem(value):
    return pltpu.with_memory_space_constraint(value, pltpu.VMEM)


def packed(value, exponent):
    scaled = value * jnp.exp2(TOP - exponent)
    return jnp.concatenate([scaled, exponent], axis=0).astype(jnp.float16)


def unpacked(value):
    value = value.astype(jnp.float32)
    exponent = value[-1:]
    return value[0:-1] * jnp.exp2(exponent - TOP), exponent


def projection_kernel(modes_hbm, snaps_hbm, *refs):
    part_refs, exponent_ref = refs[0:QUAD], refs[QUAD]
    modes, snaps, partial_sums, modes_sems, snaps_sems = refs[QUAD + 1 :]
    depth = modes.shape[0] // PROJECTION_STEPS
    quarter = snaps.shape[1] // QUAD

    def copies(step):
        at = pl.ds(step * depth, depth)
        return (
            pltpu.make_async_copy(modes_hbm.at[at], modes.at[at], modes_sems.at[step]),
            pltpu.make_async_copy(snaps_hbm.at[at], snaps.at[at], snaps_sems.at[step]),
        )

    for step in range(PROJECTION_STEPS):
        for copy in copies(step):
            copy.start()
    for step in range(PROJECTION_STEPS):
        for copy in copies(step):
            copy.wait()
        at = pl.ds(step * depth, depth)
        product = lax.dot_general(
            modes[at, :],
            snaps[at, :],
            (((0,), (0,)), ((), ())),
            preferred_element_type=jnp.float32,
        )
        if step == 0:
            partial_sums[...] = product
        else:
            partial_sums[...] += product
    largest = jnp.maximum(jnp.max(jnp.abs(partial_sums[...])), SMALLEST)
    exponent_ref[...] = jnp.floor(jnp.log2(jnp.full(exponent_ref.shape, largest)))
    place = lax.rem(lax.axis_index("space"), QUAD)
    for j in range(QUAD):
        start = pl.multiple_of(jnp.bitwise_xor(place, j) * quarter, quarter)
        part_refs[j][...] = partial_sums[:, pl.ds(start, quarter)]


def project(modes, snapshots):
    (depth, count), snaps = modes.shape, snapshots.shape[1]
    quarter = snaps // QUAD
    vmem = pl.BlockSpec(memory_space=pltpu.VMEM)
    hbm = pl.BlockSpec(memory_space=pltpu.HBM)
    *parts, exponent = pl.pallas_call(
        projection_kernel,
        out_shape=(pltpu.VMEM((count, quarter), jnp.float32),) * QUAD
        + (pltpu.VMEM((EXPONENT_ROWS, quarter), jnp.float32),),
        in_specs=[hbm] * 2,
        out_specs=(vmem,) * (QUAD + 1),
        scratch_shapes=[
            pltpu.VMEM((depth, count), jnp.bfloat16),
            pltpu.VMEM((depth, snaps), jnp.bfloat16),
            pltpu.VMEM((count, snaps), jnp.float32),
            pltpu.SemaphoreType.DMA((PROJECTION_STEPS,)),
            pltpu.SemaphoreType.DMA((PROJECTION_STEPS,)),
        ],
        compiler_params=pltpu.CompilerParams(vmem_limit_bytes=VMEM_LIMIT),
        cost_estimate=pl.CostEstimate(
            flops=2 * depth * count * snaps,
            bytes_accessed=2 * depth * (count + snaps),
            transcendentals=0,
        ),
    )(in_hbm(modes), in_hbm(snapshots))
    return [part.reshape((-1,) + exponent.shape) for part in parts], exponent[None]


def gram_kernel(sizes, *refs):
    n_time, snaps, modes, row_block, col_block, target_block, tile = sizes
    half, quarter = n_time // 2, snaps // QUAD
    count = 2 * QUAD
    pieces, (gram_hbm, rhs_hbm) = refs[0:count], refs[count : count + 2]
    lead, head, target, *rows, cols, staged, side, side_staged, sems = refs[count + 2 :]
    later = (n_time - 1) * snaps
    time_pos, space_pos = lax.axis_index("tm"), lax.axis_index("space")
    place = lax.rem(space_pos, QUAD)

    def each_piece(take):
        for other in range(2):
            for k in range(half):
                block = jnp.bitwise_xor(time_pos, 2 * k + other)
                for j in range(QUAD):
                    at = block * snaps + jnp.bitwise_xor(place, j) * quarter
                    take(pieces[other * QUAD + j].at[k], pl.multiple_of(at, quarter))

    gap = 2 * snaps
    lead[:, 0:gap] = jnp.zeros((LEAD_MODES, gap), jnp.bfloat16)
    target[:, n_time * snaps :] = jnp.zeros((target_block, snaps), jnp.bfloat16)
    wanted = pl.ds(pl.multiple_of(space_pos * target_block, ROW_TILE), target_block)

    def place_lead(piece, at):
        current = piece[0:LEAD_MODES, :]
        head[:, pl.ds(at, quarter)] = current.astype(jnp.float32)
        lead[:, pl.ds(at + gap, quarter)] = current
        target[:, pl.ds(at, quarter)] = piece[wanted, :]

    each_piece(place_lead)

    def build_group(out, q, at):
        kind, i = lax.div(q, LEAD_MODES), lax.rem(q, LEAD_MODES)
        factor = jnp.broadcast_to(head[pl.ds(i, 1), snaps:], (ROW_TILE, later)).astype(
            jnp.bfloat16
        )
        shifted = pl.ds(pl.multiple_of(gap - kind * snaps, snaps), later)
        for j in range(0, LEAD_MODES, ROW_TILE):
            out[pl.ds(pl.multiple_of(at + j, ROW_TILE), ROW_TILE), snaps:] = (
                factor * lead[j : j + ROW_TILE, shifted]
            )

    def fill(out, start, extent):
        @pl.when(start == 0)
        def _():
            def place_modes(piece, at):
                out[pl.ds(LEAD_MODES, modes), pl.ds(at, quarter)] = piece[...]

            each_piece(place_modes)

        def group(q, carry):
            build_group(out, q, modes + LEAD_MODES * q - start + LEAD_MODES)
            return carry

        first = jnp.maximum(0, lax.div(start - modes, LEAD_MODES))
        last = lax.div(start + extent - modes + LEAD_MODES - 1, LEAD_MODES)
        lax.fori_loop(first, last, group, 0)

    def fill_products(out, start, extent):
        first = lax.div(start - modes, LEAD_MODES)
        most = 2 * LEAD_MODES - 1
        for g in range(-(-(extent + LEAD_MODES - ROW_TILE) // LEAD_MODES)):
            at = modes + LEAD_MODES * (first + g) - start + LEAD_MODES
            build_group(out, jnp.minimum(first + g, most), at)

    row_start = time_pos * row_block
    fill(cols, space_pos * col_block, col_block)
    fill(rows[0], row_start, tile)
    cols[pl.ds(LEAD_MODES + col_block, target_block), snaps:] = target[:, gap:]

    def times(left, right):
        return lax.dot_general(
            left, right, (((1,), (1,)), ((), ())), preferred_element_type=jnp.float32
        ) * (1.0 / (n_time * snaps))

    first_rows = rows[0].at[pl.ds(LEAD_MODES, modes), 0:snaps]
    first_cols = cols.at[pl.ds(LEAD_MODES, modes), 0:snaps]
    writes = []
    for step in range(row_block // tile):
        top = step * tile
        at = pl.ds(top, tile)
        if top + tile < row_block:
            fill_products(rows[(step + 1) % 2], row_start + top + tile, tile)
        product = times(
            rows[step % 2][pl.ds(LEAD_MODES, tile), snaps:],
            cols[pl.ds(LEAD_MODES, col_block + target_block), snaps:],
        )
        shape = (tile, col_block)
        row = time_pos * row_block + top + lax.broadcasted_iota(jnp.int32, shape, 0)
        column = space_pos * col_block + lax.broadcasted_iota(jnp.int32, shape, 1)
        staged[at, :] = product[:, 0:col_block] + jnp.where(row == column, RIDGE_WEIGHT, 0.0)
        side[at, :] = product[:, col_block:]
        if step == 0:

            @pl.when(time_pos == 0)
            def _():
                side[0:modes, :] += times(first_rows[...], target[:, snaps:gap])

            @pl.when((time_pos == 0) & (space_pos == 0))
            def _():
                staged[0:modes, 0:modes] += times(
                    first_rows[...], first_cols[...]
                )

        writes.append(pltpu.make_async_copy(staged.at[at], gram_hbm.at[at], sems.at[step]))
        writes[-1].start()
    side_staged[...] = side[...].T
    writes.append(pltpu.make_async_copy(side_staged, rhs_hbm, sems.at[len(writes)]))
    writes[-1].start()
    for write in writes:
        write.wait()


def gram_blocks(pieces, n_time, n_space):
    _, modes, quarter = pieces[0].shape
    snaps = QUAD * quarter
    features = modes + 2 * LEAD_MODES * LEAD_MODES
    row_block, col_block, target_block = features // n_time, features // n_space, modes // n_space
    later = (n_time - 1) * snaps
    tile = row_block // 4 if row_block % (4 * ROW_TILE) == 0 else row_block
    assert min(tile, col_block) >= modes
    vmem = pl.BlockSpec(memory_space=pltpu.VMEM)
    gram, rhs = pl.pallas_call(
        functools.partial(
            gram_kernel, (n_time, snaps, modes, row_block, col_block, target_block, tile)
        ),
        out_shape=(
            jax.ShapeDtypeStruct((row_block, col_block), jnp.float32),
            jax.ShapeDtypeStruct((target_block, row_block), jnp.float32),
        ),
        in_specs=[vmem] * len(pieces),
        out_specs=(pl.BlockSpec(memory_space=pl.ANY),) * 2,
        scratch_shapes=[
            pltpu.VMEM((LEAD_MODES, (n_time + 2) * snaps), jnp.bfloat16),
            pltpu.VMEM((LEAD_MODES, n_time * snaps), jnp.float32),
            pltpu.VMEM((target_block, (n_time + 1) * snaps), jnp.bfloat16),
            pltpu.VMEM((tile + 2 * LEAD_MODES, n_time * snaps), jnp.bfloat16),
            pltpu.VMEM((tile + 2 * LEAD_MODES, n_time * snaps), jnp.bfloat16),
            pltpu.VMEM((col_block + 2 * LEAD_MODES + target_block, n_time * snaps), jnp.bfloat16),
            pltpu.VMEM((row_block, col_block), jnp.float32),
            pltpu.VMEM((row_block, target_block), jnp.float32),
            pltpu.VMEM((target_block, row_block), jnp.float32),
            pltpu.SemaphoreType.DMA((row_block // tile + 1,)),
        ],
        compiler_params=pltpu.CompilerParams(vmem_limit_bytes=VMEM_LIMIT),
        cost_estimate=pl.CostEstimate(
            flops=2 * row_block * (col_block + target_block) * later,
            bytes_accessed=4 * row_block * (col_block + target_block),
            transcendentals=0,
        ),
    )(*map(in_vmem, pieces))
    return gram, rhs.T


def joined(value, axis, bit):
    return jnp.concatenate([value, swap(value, axis, bit)], axis=0)


def per_device(snapshots, modes):
    n_space, n_time = lax.axis_size("space"), lax.axis_size("tm")
    (mine, *others), exponent = project(modes, snapshots)
    arrived = [swap(packed(part, exponent), "space", j) for j, part in enumerate(others, 1)]
    for part in arrived:
        value, scale = unpacked(part)
        mine, exponent = mine + value, jnp.maximum(exponent, scale)
    for bit in bits_of(n_space)[2:]:
        out = packed(mine, exponent)
        (mine, own), (value, scale) = unpacked(out), unpacked(swap(out, "space", bit))
        mine, exponent = mine + value, jnp.maximum(own, scale)
    mine = mine.astype(jnp.bfloat16).reshape(1, modes.shape[1], -1)
    for bit in bits_of(n_time)[1:]:
        mine = joined(mine, "tm", bit)
    pieces = [mine] + [swap(mine, "space", j) for j in range(1, QUAD)]
    pieces = pieces + [swap(piece, "tm", 1) for piece in pieces]
    return gram_blocks(pieces, n_time, n_space)


def solution(mesh):
    in_specs = (P("space", "tm"), P("space", None))
    out_specs = (P("tm", "space"), P("tm", "space"))
    return jax.shard_map(
        per_device, mesh=mesh, in_specs=in_specs, out_specs=out_specs, check_vma=False
    )
```

```python
import functools

import jax
import jax.numpy as jnp
from jax import lax
from jax.experimental import pallas as pl
from jax.experimental.pallas import tpu as pltpu
from jax.sharding import PartitionSpec as P

LEAD_MODES = 48
RIDGE_WEIGHT = 0.05
ROW_TILE = 16
QUAD = 4
SUM_PARTNERS = ((0, 3, 2, 1), (0, 3, 1, 2))
GATHER_PARTNERS = ((0, 2, 3, 1), (0, 3, 2, 1))
PROJECTION_STEPS = 10
EXPONENT_ROWS = 8
TOP = 9.0
SMALLEST = 1e-30
VMEM_LIMIT = 48 * 2**20


def swap(value, axis, bit):
    count = lax.axis_size(axis)
    return lax.ppermute(value, axis, [(i, i ^ bit) for i in range(count)])


def swap_quad(value, partners, turn):
    n_space, n_time = lax.axis_size("space"), lax.axis_size("tm")
    pairs = [
        (s * n_time + t, (s ^ partners[t % 2][turn]) * n_time + t)
        for s in range(n_space)
        for t in range(n_time)
    ]
    return lax.ppermute(value, ("space", "tm"), pairs)


def partner(partners, core, turn):
    even, odd = partners[0][turn], partners[1][turn]
    return even if even == odd else jnp.where(core == 0, even, odd)


def bits_of(count):
    return [1 << k for k in range(count.bit_length() - 1)]


def in_hbm(value):
    return pltpu.with_memory_space_constraint(value, pltpu.HBM)


def in_vmem(value):
    return pltpu.with_memory_space_constraint(value, pltpu.VMEM)


def packed(value, exponent):
    scaled = value * jnp.exp2(TOP - exponent)
    return jnp.concatenate([scaled, exponent], axis=0).astype(jnp.float16)


def unpacked(value):
    value = value.astype(jnp.float32)
    exponent = value[-1:]
    return value[0:-1] * jnp.exp2(exponent - TOP), exponent


def projection_kernel(modes_hbm, snaps_hbm, *refs):
    part_refs, exponent_ref = refs[0:QUAD], refs[QUAD]
    modes, snaps, partial_sums, modes_sems, snaps_sems = refs[QUAD + 1 :]
    depth = modes.shape[0] // PROJECTION_STEPS
    quarter = snaps.shape[1] // QUAD

    def copies(step):
        at = pl.ds(step * depth, depth)
        return (
            pltpu.make_async_copy(modes_hbm.at[at], modes.at[at], modes_sems.at[step]),
            pltpu.make_async_copy(snaps_hbm.at[at], snaps.at[at], snaps_sems.at[step]),
        )

    for step in range(PROJECTION_STEPS):
        for copy in copies(step):
            copy.start()
    for step in range(PROJECTION_STEPS):
        for copy in copies(step):
            copy.wait()
        at = pl.ds(step * depth, depth)
        product = lax.dot_general(
            modes[at, :],
            snaps[at, :],
            (((0,), (0,)), ((), ())),
            preferred_element_type=jnp.float32,
        )
        if step == 0:
            partial_sums[...] = product
        else:
            partial_sums[...] += product
    largest = jnp.maximum(jnp.max(jnp.abs(partial_sums[...])), SMALLEST)
    exponent_ref[...] = jnp.floor(jnp.log2(jnp.full(exponent_ref.shape, largest)))
    place = lax.rem(lax.axis_index("space"), QUAD)
    core = lax.rem(lax.axis_index("tm"), 2)
    for j in range(QUAD):
        start = pl.multiple_of(jnp.bitwise_xor(place, partner(SUM_PARTNERS, core, j)) * quarter, quarter)
        part_refs[j][...] = partial_sums[:, pl.ds(start, quarter)]


def project(modes, snapshots):
    (depth, count), snaps = modes.shape, snapshots.shape[1]
    quarter = snaps // QUAD
    vmem = pl.BlockSpec(memory_space=pltpu.VMEM)
    hbm = pl.BlockSpec(memory_space=pltpu.HBM)
    *parts, exponent = pl.pallas_call(
        projection_kernel,
        out_shape=(pltpu.VMEM((count, quarter), jnp.float32),) * QUAD
        + (pltpu.VMEM((EXPONENT_ROWS, quarter), jnp.float32),),
        in_specs=[hbm] * 2,
        out_specs=(vmem,) * (QUAD + 1),
        scratch_shapes=[
            pltpu.VMEM((depth, count), jnp.bfloat16),
            pltpu.VMEM((depth, snaps), jnp.bfloat16),
            pltpu.VMEM((count, snaps), jnp.float32),
            pltpu.SemaphoreType.DMA((PROJECTION_STEPS,)),
            pltpu.SemaphoreType.DMA((PROJECTION_STEPS,)),
        ],
        compiler_params=pltpu.CompilerParams(vmem_limit_bytes=VMEM_LIMIT),
        cost_estimate=pl.CostEstimate(
            flops=2 * depth * count * snaps,
            bytes_accessed=2 * depth * (count + snaps),
            transcendentals=0,
        ),
    )(in_hbm(modes), in_hbm(snapshots))
    return [part.reshape((-1,) + exponent.shape) for part in parts], exponent[None]


def gram_kernel(sizes, *refs):
    n_time, snaps, modes, row_block, col_block, target_block, tile = sizes
    half, quarter = n_time // 2, snaps // QUAD
    count = 2 * QUAD
    pieces, (gram_hbm, rhs_hbm) = refs[0:count], refs[count : count + 2]
    lead, head, target, *rows, cols, staged, side, side_staged, sems = refs[count + 2 :]
    later = (n_time - 1) * snaps
    time_pos, space_pos = lax.axis_index("tm"), lax.axis_index("space")
    place, core = lax.rem(space_pos, QUAD), lax.rem(time_pos, 2)

    def each_piece(take):
        for other in range(2):
            for k in range(half):
                block = jnp.bitwise_xor(time_pos, 2 * k + other)
                for j in range(QUAD):
                    source = partner(GATHER_PARTNERS, jnp.bitwise_xor(core, other), j)
                    at = block * snaps + jnp.bitwise_xor(place, source) * quarter
                    take(pieces[other * QUAD + j].at[k], pl.multiple_of(at, quarter))

    gap = 2 * snaps
    lead[:, 0:gap] = jnp.zeros((LEAD_MODES, gap), jnp.bfloat16)
    target[:, n_time * snaps :] = jnp.zeros((target_block, snaps), jnp.bfloat16)
    wanted = pl.ds(pl.multiple_of(space_pos * target_block, ROW_TILE), target_block)

    def place_lead(piece, at):
        current = piece[0:LEAD_MODES, :]
        head[:, pl.ds(at, quarter)] = current.astype(jnp.float32)
        lead[:, pl.ds(at + gap, quarter)] = current
        target[:, pl.ds(at, quarter)] = piece[wanted, :]

    each_piece(place_lead)

    def build_group(out, q, at):
        kind, i = lax.div(q, LEAD_MODES), lax.rem(q, LEAD_MODES)
        factor = jnp.broadcast_to(head[pl.ds(i, 1), snaps:], (ROW_TILE, later)).astype(
            jnp.bfloat16
        )
        shifted = pl.ds(pl.multiple_of(gap - kind * snaps, snaps), later)
        for j in range(0, LEAD_MODES, ROW_TILE):
            out[pl.ds(pl.multiple_of(at + j, ROW_TILE), ROW_TILE), snaps:] = (
                factor * lead[j : j + ROW_TILE, shifted]
            )

    def fill(out, start, extent):
        @pl.when(start == 0)
        def _():
            def place_modes(piece, at):
                out[pl.ds(LEAD_MODES, modes), pl.ds(at, quarter)] = piece[...]

            each_piece(place_modes)

        def group(q, carry):
            build_group(out, q, modes + LEAD_MODES * q - start + LEAD_MODES)
            return carry

        first = jnp.maximum(0, lax.div(start - modes, LEAD_MODES))
        last = lax.div(start + extent - modes + LEAD_MODES - 1, LEAD_MODES)
        lax.fori_loop(first, last, group, 0)

    def fill_products(out, start, extent):
        first = lax.div(start - modes, LEAD_MODES)
        most = 2 * LEAD_MODES - 1
        for g in range(-(-(extent + LEAD_MODES - ROW_TILE) // LEAD_MODES)):
            at = modes + LEAD_MODES * (first + g) - start + LEAD_MODES
            build_group(out, jnp.minimum(first + g, most), at)

    row_start = time_pos * row_block
    fill(cols, space_pos * col_block, col_block)
    fill(rows[0], row_start, tile)
    cols[pl.ds(LEAD_MODES + col_block, target_block), snaps:] = target[:, gap:]

    def times(left, right):
        return lax.dot_general(
            left, right, (((1,), (1,)), ((), ())), preferred_element_type=jnp.float32
        ) * (1.0 / (n_time * snaps))

    first_rows = rows[0].at[pl.ds(LEAD_MODES, modes), 0:snaps]
    first_cols = cols.at[pl.ds(LEAD_MODES, modes), 0:snaps]
    writes = []
    for step in range(row_block // tile):
        top = step * tile
        at = pl.ds(top, tile)
        if top + tile < row_block:
            fill_products(rows[(step + 1) % 2], row_start + top + tile, tile)
        product = times(
            rows[step % 2][pl.ds(LEAD_MODES, tile), snaps:],
            cols[pl.ds(LEAD_MODES, col_block + target_block), snaps:],
        )
        shape = (tile, col_block)
        row = time_pos * row_block + top + lax.broadcasted_iota(jnp.int32, shape, 0)
        column = space_pos * col_block + lax.broadcasted_iota(jnp.int32, shape, 1)
        staged[at, :] = product[:, 0:col_block] + jnp.where(row == column, RIDGE_WEIGHT, 0.0)
        side[at, :] = product[:, col_block:]
        if step == 0:

            @pl.when(time_pos == 0)
            def _():
                side[0:modes, :] += times(first_rows[...], target[:, snaps:gap])

            @pl.when((time_pos == 0) & (space_pos == 0))
            def _():
                staged[0:modes, 0:modes] += times(
                    first_rows[...], first_cols[...]
                )

        writes.append(pltpu.make_async_copy(staged.at[at], gram_hbm.at[at], sems.at[step]))
        writes[-1].start()
    side_staged[...] = side[...].T
    writes.append(pltpu.make_async_copy(side_staged, rhs_hbm, sems.at[len(writes)]))
    writes[-1].start()
    for write in writes:
        write.wait()


def gram_blocks(pieces, n_time, n_space):
    _, modes, quarter = pieces[0].shape
    snaps = QUAD * quarter
    features = modes + 2 * LEAD_MODES * LEAD_MODES
    row_block, col_block, target_block = features // n_time, features // n_space, modes // n_space
    later = (n_time - 1) * snaps
    tile = row_block // 4 if row_block % (4 * ROW_TILE) == 0 else row_block
    assert min(tile, col_block) >= modes
    vmem = pl.BlockSpec(memory_space=pltpu.VMEM)
    gram, rhs = pl.pallas_call(
        functools.partial(
            gram_kernel, (n_time, snaps, modes, row_block, col_block, target_block, tile)
        ),
        out_shape=(
            jax.ShapeDtypeStruct((row_block, col_block), jnp.float32),
            jax.ShapeDtypeStruct((target_block, row_block), jnp.float32),
        ),
        in_specs=[vmem] * len(pieces),
        out_specs=(pl.BlockSpec(memory_space=pl.ANY),) * 2,
        scratch_shapes=[
            pltpu.VMEM((LEAD_MODES, (n_time + 2) * snaps), jnp.bfloat16),
            pltpu.VMEM((LEAD_MODES, n_time * snaps), jnp.float32),
            pltpu.VMEM((target_block, (n_time + 1) * snaps), jnp.bfloat16),
            pltpu.VMEM((tile + 2 * LEAD_MODES, n_time * snaps), jnp.bfloat16),
            pltpu.VMEM((tile + 2 * LEAD_MODES, n_time * snaps), jnp.bfloat16),
            pltpu.VMEM((col_block + 2 * LEAD_MODES + target_block, n_time * snaps), jnp.bfloat16),
            pltpu.VMEM((row_block, col_block), jnp.float32),
            pltpu.VMEM((row_block, target_block), jnp.float32),
            pltpu.VMEM((target_block, row_block), jnp.float32),
            pltpu.SemaphoreType.DMA((row_block // tile + 1,)),
        ],
        compiler_params=pltpu.CompilerParams(vmem_limit_bytes=VMEM_LIMIT),
        cost_estimate=pl.CostEstimate(
            flops=2 * row_block * (col_block + target_block) * later,
            bytes_accessed=4 * row_block * (col_block + target_block),
            transcendentals=0,
        ),
    )(*map(in_vmem, pieces))
    return gram, rhs.T


def joined(value, axis, bit):
    return jnp.concatenate([value, swap(value, axis, bit)], axis=0)


def per_device(snapshots, modes):
    n_space, n_time = lax.axis_size("space"), lax.axis_size("tm")
    (mine, *others), exponent = project(modes, snapshots)
    arrived = [swap_quad(packed(part, exponent), SUM_PARTNERS, j) for j, part in enumerate(others, 1)]
    for part in arrived:
        value, scale = unpacked(part)
        mine, exponent = mine + value, jnp.maximum(exponent, scale)
    for bit in bits_of(n_space)[2:]:
        out = packed(mine, exponent)
        (mine, own), (value, scale) = unpacked(out), unpacked(swap(out, "space", bit))
        mine, exponent = mine + value, jnp.maximum(own, scale)
    mine = mine.astype(jnp.bfloat16).reshape(1, modes.shape[1], -1)
    for bit in bits_of(n_time)[1:]:
        mine = joined(mine, "tm", bit)
    pieces = [mine] + [swap_quad(mine, GATHER_PARTNERS, j) for j in range(1, QUAD)]
    pieces = pieces + [swap(piece, "tm", 1) for piece in pieces]
    return gram_blocks(pieces, n_time, n_space)


def solution(mesh):
    in_specs = (P("space", "tm"), P("space", None))
    out_specs = (P("tm", "space"), P("tm", "space"))
    return jax.shard_map(
        per_device, mesh=mesh, in_specs=in_specs, out_specs=out_specs, check_vma=False
    )
```

```python
import functools

import jax
import jax.numpy as jnp
from jax import lax
from jax.experimental import pallas as pl
from jax.experimental.pallas import tpu as pltpu
from jax.sharding import PartitionSpec as P

LEAD_MODES = 48
RIDGE_WEIGHT = 0.05
ROW_TILE = 16
QUAD = 4
SUM_PARTNERS = ((0, 3, 2, 1), (0, 3, 1, 2))
GATHER_PARTNERS = ((0, 2, 3, 1), (0, 3, 2, 1))
PROJECTION_STEPS = 10
EXPONENT_ROWS = 8
TOP = 9.0
SMALLEST = 1e-30
VMEM_LIMIT = 48 * 2**20
GRAM_VMEM_LIMIT = 32 * 2**20
EAGERNESS = 20


def swap(value, axis, bit):
    count = lax.axis_size(axis)
    return lax.ppermute(value, axis, [(i, i ^ bit) for i in range(count)])


def swap_quad(value, partners, turn):
    n_space, n_time = lax.axis_size("space"), lax.axis_size("tm")
    pairs = [
        (s * n_time + t, (s ^ partners[t % 2][turn]) * n_time + t)
        for s in range(n_space)
        for t in range(n_time)
    ]
    return lax.ppermute(value, ("space", "tm"), pairs)


def partner(partners, core, turn):
    even, odd = partners[0][turn], partners[1][turn]
    return even if even == odd else jnp.where(core == 0, even, odd)


def bits_of(count):
    return [1 << k for k in range(count.bit_length() - 1)]


def in_hbm(value):
    return pltpu.with_memory_space_constraint(value, pltpu.HBM)


def in_vmem(value):
    return pltpu.with_memory_space_constraint(value, pltpu.VMEM)


def packed(value, exponent):
    scaled = value * jnp.exp2(TOP - exponent)
    return jnp.concatenate([scaled, exponent], axis=0).astype(jnp.float16)


def unpacked(value):
    value = value.astype(jnp.float32)
    exponent = value[-1:]
    return value[0:-1] * jnp.exp2(exponent - TOP), exponent


def projection_kernel(modes_hbm, snaps_hbm, *refs):
    part_refs, exponent_ref = refs[0:QUAD], refs[QUAD]
    modes, snaps, partial_sums, modes_sems, snaps_sems = refs[QUAD + 1 :]
    depth = modes.shape[0] // PROJECTION_STEPS
    quarter = snaps.shape[1] // QUAD

    def copies(step):
        at = pl.ds(step * depth, depth)
        return (
            pltpu.make_async_copy(modes_hbm.at[at], modes.at[at], modes_sems.at[step]),
            pltpu.make_async_copy(snaps_hbm.at[at], snaps.at[at], snaps_sems.at[step]),
        )

    for step in range(PROJECTION_STEPS):
        for copy in copies(step):
            copy.start()
    for step in range(PROJECTION_STEPS):
        for copy in copies(step):
            copy.wait()
        at = pl.ds(step * depth, depth)
        product = lax.dot_general(
            modes[at, :],
            snaps[at, :],
            (((0,), (0,)), ((), ())),
            preferred_element_type=jnp.float32,
        )
        if step == 0:
            partial_sums[...] = product
        else:
            partial_sums[...] += product
    largest = jnp.maximum(jnp.max(jnp.abs(partial_sums[...])), SMALLEST)
    exponent_ref[...] = jnp.floor(jnp.log2(jnp.full(exponent_ref.shape, largest)))
    place = lax.rem(lax.axis_index("space"), QUAD)
    core = lax.rem(lax.axis_index("tm"), 2)
    for j in range(QUAD):
        start = pl.multiple_of(jnp.bitwise_xor(place, partner(SUM_PARTNERS, core, j)) * quarter, quarter)
        part_refs[j][...] = partial_sums[:, pl.ds(start, quarter)]


def project(modes, snapshots):
    (depth, count), snaps = modes.shape, snapshots.shape[1]
    quarter = snaps // QUAD
    vmem = pl.BlockSpec(memory_space=pltpu.VMEM)
    hbm = pl.BlockSpec(memory_space=pltpu.HBM)
    *parts, exponent = pl.pallas_call(
        projection_kernel,
        out_shape=(pltpu.VMEM((count, quarter), jnp.float32),) * QUAD
        + (pltpu.VMEM((EXPONENT_ROWS, quarter), jnp.float32),),
        in_specs=[hbm] * 2,
        out_specs=(vmem,) * (QUAD + 1),
        scratch_shapes=[
            pltpu.VMEM((depth, count), jnp.bfloat16),
            pltpu.VMEM((depth, snaps), jnp.bfloat16),
            pltpu.VMEM((count, snaps), jnp.float32),
            pltpu.SemaphoreType.DMA((PROJECTION_STEPS,)),
            pltpu.SemaphoreType.DMA((PROJECTION_STEPS,)),
        ],
        compiler_params=pltpu.CompilerParams(vmem_limit_bytes=VMEM_LIMIT),
        cost_estimate=pl.CostEstimate(
            flops=2 * depth * count * snaps,
            bytes_accessed=2 * depth * (count + snaps),
            transcendentals=0,
        ),
    )(in_hbm(modes), in_hbm(snapshots))
    return [part.reshape((-1,) + exponent.shape) for part in parts], exponent[None]


def gram_kernel(sizes, turns, *refs):
    n_time, quarter, modes, row_block, col_block, target_block, tile = sizes
    half, snaps, is_last = n_time // 2, quarter * len(turns), 0 not in turns
    refs = list(refs)

    def taken(count):
        return [refs.pop(0) for _ in range(count)]

    pieces = taken(2 * len(turns))
    (before,) = taken(1) if is_last else (None,)
    outs = taken(2 if is_last else 1)
    lead, head, target, *rows, cols = taken(6)
    if is_last:
        (gram_hbm, rhs_hbm), (staged, side, side_staged, sems) = outs, refs
        scale = 1.0 / (n_time * QUAD * quarter)
    else:
        staged = side = outs[0]
        scale = 1.0
    aside = slice(0, target_block) if is_last else slice(col_block, col_block + target_block)
    later = (n_time - 1) * snaps
    time_pos, space_pos = lax.axis_index("tm"), lax.axis_index("space")
    core = lax.rem(time_pos, 2)

    def each_piece(take):
        for other in range(2):
            for k in range(half):
                block = jnp.bitwise_xor(time_pos, 2 * k + other)
                for j, turn in enumerate(turns):
                    source = partner(GATHER_PARTNERS, jnp.bitwise_xor(core, other), turn)
                    at = block * snaps + (source - min(turns)) * quarter
                    piece = pieces[other * len(turns) + j].at[k]
                    take(piece, pl.multiple_of(at, quarter))

    gap = 2 * snaps
    lead[:, 0:gap] = jnp.zeros((LEAD_MODES, gap), jnp.bfloat16)
    target[:, n_time * snaps :] = jnp.zeros((target_block, snaps), jnp.bfloat16)
    wanted = pl.ds(pl.multiple_of(space_pos * target_block, ROW_TILE), target_block)

    def place_lead(piece, at):
        current = piece[0:LEAD_MODES, :]
        head[:, pl.ds(at, quarter)] = current.astype(jnp.float32)
        lead[:, pl.ds(at + gap, quarter)] = current
        target[:, pl.ds(at, quarter)] = piece[wanted, :]

    each_piece(place_lead)

    def build_group(out, q, at):
        kind, i = lax.div(q, LEAD_MODES), lax.rem(q, LEAD_MODES)
        factor = jnp.broadcast_to(head[pl.ds(i, 1), snaps:], (ROW_TILE, later)).astype(
            jnp.bfloat16
        )
        shifted = pl.ds(pl.multiple_of(gap - kind * snaps, snaps), later)
        for j in range(0, LEAD_MODES, ROW_TILE):
            out[pl.ds(pl.multiple_of(at + j, ROW_TILE), ROW_TILE), snaps:] = (
                factor * lead[j : j + ROW_TILE, shifted]
            )

    def fill(out, start, extent):
        @pl.when(start == 0)
        def _():
            def place_modes(piece, at):
                out[pl.ds(LEAD_MODES, modes), pl.ds(at, quarter)] = piece[...]

            each_piece(place_modes)

        def group(q, carry):
            build_group(out, q, modes + LEAD_MODES * q - start + LEAD_MODES)
            return carry

        first = jnp.maximum(0, lax.div(start - modes, LEAD_MODES))
        last = lax.div(start + extent - modes + LEAD_MODES - 1, LEAD_MODES)
        lax.fori_loop(first, last, group, 0)

    def fill_products(out, start, extent):
        first = lax.div(start - modes, LEAD_MODES)
        most = 2 * LEAD_MODES - 1
        for g in range(-(-(extent + LEAD_MODES - ROW_TILE) // LEAD_MODES)):
            at = modes + LEAD_MODES * (first + g) - start + LEAD_MODES
            build_group(out, jnp.minimum(first + g, most), at)

    row_start = time_pos * row_block
    fill(cols, space_pos * col_block, col_block)
    fill(rows[0], row_start, tile)
    cols[pl.ds(LEAD_MODES + col_block, target_block), snaps:] = target[:, gap:]

    def times(left, right):
        return lax.dot_general(
            left, right, (((1,), (1,)), ((), ())), preferred_element_type=jnp.float32
        )

    first_rows = rows[0].at[pl.ds(LEAD_MODES, modes), 0:snaps]
    first_cols = cols.at[pl.ds(LEAD_MODES, modes), 0:snaps]
    writes = []
    for step in range(row_block // tile):
        top = step * tile
        at = pl.ds(top, tile)
        if top + tile < row_block:
            fill_products(rows[(step + 1) % 2], row_start + top + tile, tile)
        product = times(
            rows[step % 2][pl.ds(LEAD_MODES, tile), snaps:],
            cols[pl.ds(LEAD_MODES, col_block + target_block), snaps:],
        )
        if is_last:
            product = (product + before[at, :]) * scale
        shape = (tile, col_block)
        row = time_pos * row_block + top + lax.broadcasted_iota(jnp.int32, shape, 0)
        column = space_pos * col_block + lax.broadcasted_iota(jnp.int32, shape, 1)
        if is_last:
            ridge = jnp.where(row == column, RIDGE_WEIGHT, 0.0)
            staged[at, :] = product[:, 0:col_block] + ridge
            side[at, :] = product[:, col_block:]
        else:
            staged[at, :] = product
        if step == 0:

            @pl.when(time_pos == 0)
            def _():
                extra = times(first_rows[...], target[:, snaps:gap]) * scale
                side[0:modes, aside] += extra

            @pl.when((time_pos == 0) & (space_pos == 0))
            def _():
                extra = times(first_rows[...], first_cols[...]) * scale
                staged[0:modes, 0:modes] += extra

        if not is_last:
            continue
        writes.append(pltpu.make_async_copy(staged.at[at], gram_hbm.at[at], sems.at[step]))
        writes[-1].start()
    if not is_last:
        return
    side_staged[...] = side[...].T
    writes.append(pltpu.make_async_copy(side_staged, rhs_hbm, sems.at[len(writes)]))
    writes[-1].start()
    for write in writes:
        write.wait()


def add_quarters(turns, pieces, before, n_time, n_space):
    _, modes, quarter = pieces[0].shape
    features = modes + 2 * LEAD_MODES * LEAD_MODES
    row_block, col_block, target_block = features // n_time, features // n_space, modes // n_space
    tile = row_block // 4 if row_block % (4 * ROW_TILE) == 0 else row_block
    assert min(tile, col_block) >= modes
    snaps, is_last = quarter * len(turns), before is not None
    width = col_block + target_block
    total = n_time * snaps
    scratch = [
        pltpu.VMEM((LEAD_MODES, total + 2 * snaps), jnp.bfloat16),
        pltpu.VMEM((LEAD_MODES, total), jnp.float32),
        pltpu.VMEM((target_block, total + snaps), jnp.bfloat16),
        pltpu.VMEM((tile + 2 * LEAD_MODES, total), jnp.bfloat16),
        pltpu.VMEM((tile + 2 * LEAD_MODES, total), jnp.bfloat16),
        pltpu.VMEM((width + 2 * LEAD_MODES, total), jnp.bfloat16),
    ]
    vmem = pl.BlockSpec(memory_space=pltpu.VMEM)
    if is_last:
        out_shape = (
            jax.ShapeDtypeStruct((row_block, col_block), jnp.float32),
            jax.ShapeDtypeStruct((target_block, row_block), jnp.float32),
        )
        out_specs = (pl.BlockSpec(memory_space=pl.ANY),) * 2
        scratch += [
            pltpu.VMEM((row_block, col_block), jnp.float32),
            pltpu.VMEM((row_block, target_block), jnp.float32),
            pltpu.VMEM((target_block, row_block), jnp.float32),
            pltpu.SemaphoreType.DMA((row_block // tile + 1,)),
        ]
    else:
        out_shape, out_specs = pltpu.VMEM((row_block, width), jnp.float32), vmem
    operands = pieces + ([before] if is_last else [])
    return pl.pallas_call(
        functools.partial(
            gram_kernel,
            (n_time, quarter, modes, row_block, col_block, target_block, tile),
            turns,
        ),
        out_shape=out_shape,
        in_specs=[vmem] * len(operands),
        out_specs=out_specs,
        scratch_shapes=scratch,
        compiler_params=pltpu.CompilerParams(vmem_limit_bytes=GRAM_VMEM_LIMIT),
        cost_estimate=pl.CostEstimate(
            flops=EAGERNESS * row_block * width * total,
            bytes_accessed=4 * row_block * width,
            transcendentals=0,
        ),
    )(*map(in_vmem, operands))


def joined(value, axis, bit):
    return jnp.concatenate([value, swap(value, axis, bit)], axis=0)


def per_device(snapshots, modes):
    n_space, n_time = lax.axis_size("space"), lax.axis_size("tm")
    (mine, *others), exponent = project(modes, snapshots)
    arrived = [swap_quad(packed(part, exponent), SUM_PARTNERS, j) for j, part in enumerate(others, 1)]
    for part in arrived:
        value, scale = unpacked(part)
        mine, exponent = mine + value, jnp.maximum(exponent, scale)
    for bit in bits_of(n_space)[2:]:
        out = packed(mine, exponent)
        (mine, own), (value, scale) = unpacked(out), unpacked(swap(out, "space", bit))
        mine, exponent = mine + value, jnp.maximum(own, scale)
    mine = mine.astype(jnp.bfloat16).reshape(1, modes.shape[1], -1)
    for bit in bits_of(n_time)[1:]:
        mine = joined(mine, "tm", bit)
    others = [swap_quad(mine, GATHER_PARTNERS, j) for j in range(1, QUAD)]
    total = add_quarters((0,), [mine, swap(mine, "tm", 1)], None, n_time, n_space)
    pieces = others + [swap(piece, "tm", 1) for piece in others]
    gram, rhs = add_quarters((1, 2, 3), pieces, total, n_time, n_space)
    return gram, rhs.T


def solution(mesh):
    in_specs = (P("space", "tm"), P("space", None))
    out_specs = (P("tm", "space"), P("tm", "space"))
    return jax.shard_map(
        per_device, mesh=mesh, in_specs=in_specs, out_specs=out_specs, check_vma=False
    )
```

```python
import functools

import jax
import jax.numpy as jnp
from jax import lax
from jax.experimental import pallas as pl
from jax.experimental.pallas import tpu as pltpu
from jax.sharding import PartitionSpec as P

LEAD_MODES = 48
RIDGE_WEIGHT = 0.05
ROW_TILE = 16
QUAD = 4
SUM_PARTNERS = ((0, 3, 2, 1), (0, 3, 1, 2))
GATHER_PARTNERS = ((0, 2, 3, 1), (0, 3, 2, 1))
PROJECTION_STEPS = 10
EXPONENT_ROWS = 8
TOP = 9.0
SMALLEST = 1e-30
VMEM_LIMIT = 48 * 2**20
GRAM_VMEM_LIMIT = 32 * 2**20
EAGERNESS = 20


def swap(value, axis, bit):
    count = lax.axis_size(axis)
    return lax.ppermute(value, axis, [(i, i ^ bit) for i in range(count)])


def swap_quad(value, partners, turn):
    n_space, n_time = lax.axis_size("space"), lax.axis_size("tm")
    pairs = [
        (s * n_time + t, (s ^ partners[t % 2][turn]) * n_time + t)
        for s in range(n_space)
        for t in range(n_time)
    ]
    return lax.ppermute(value, ("space", "tm"), pairs)


def partner(partners, core, turn):
    even, odd = partners[0][turn], partners[1][turn]
    return even if even == odd else jnp.where(core == 0, even, odd)


def bits_of(count):
    return [1 << k for k in range(count.bit_length() - 1)]


def in_hbm(value):
    return pltpu.with_memory_space_constraint(value, pltpu.HBM)


def in_vmem(value):
    return pltpu.with_memory_space_constraint(value, pltpu.VMEM)


def packed(value, exponent):
    scaled = value * jnp.exp2(TOP - exponent)
    return jnp.concatenate([scaled, exponent], axis=0).astype(jnp.float16)


def unpacked(value):
    value = value.astype(jnp.float32)
    exponent = value[-1:]
    return value[0:-1] * jnp.exp2(exponent - TOP), exponent


def projection_kernel(modes_hbm, snaps_hbm, *refs):
    part_refs, exponent_ref = refs[0:QUAD], refs[QUAD]
    modes, snaps, partial_sums, modes_sems, snaps_sems = refs[QUAD + 1 :]
    depth = modes.shape[0] // PROJECTION_STEPS
    quarter = snaps.shape[1] // QUAD

    def copies(step):
        at = pl.ds(step * depth, depth)
        return (
            pltpu.make_async_copy(modes_hbm.at[at], modes.at[at], modes_sems.at[step]),
            pltpu.make_async_copy(snaps_hbm.at[at], snaps.at[at], snaps_sems.at[step]),
        )

    for step in range(PROJECTION_STEPS):
        for copy in copies(step):
            copy.start()
    for step in range(PROJECTION_STEPS):
        for copy in copies(step):
            copy.wait()
        at = pl.ds(step * depth, depth)
        product = lax.dot_general(
            modes[at, :],
            snaps[at, :],
            (((0,), (0,)), ((), ())),
            preferred_element_type=jnp.float32,
        )
        if step == 0:
            partial_sums[...] = product
        else:
            partial_sums[...] += product
    largest = jnp.maximum(jnp.max(jnp.abs(partial_sums[...])), SMALLEST)
    exponent_ref[...] = jnp.floor(jnp.log2(jnp.full(exponent_ref.shape, largest)))
    place = lax.rem(lax.axis_index("space"), QUAD)
    core = lax.rem(lax.axis_index("tm"), 2)
    for j in range(QUAD):
        start = pl.multiple_of(jnp.bitwise_xor(place, partner(SUM_PARTNERS, core, j)) * quarter, quarter)
        part_refs[j][...] = partial_sums[:, pl.ds(start, quarter)]


def project(modes, snapshots):
    (depth, count), snaps = modes.shape, snapshots.shape[1]
    quarter = snaps // QUAD
    vmem = pl.BlockSpec(memory_space=pltpu.VMEM)
    hbm = pl.BlockSpec(memory_space=pltpu.HBM)
    *parts, exponent = pl.pallas_call(
        projection_kernel,
        out_shape=(pltpu.VMEM((count, quarter), jnp.float32),) * QUAD
        + (pltpu.VMEM((EXPONENT_ROWS, quarter), jnp.float32),),
        in_specs=[hbm] * 2,
        out_specs=(vmem,) * (QUAD + 1),
        scratch_shapes=[
            pltpu.VMEM((depth, count), jnp.bfloat16),
            pltpu.VMEM((depth, snaps), jnp.bfloat16),
            pltpu.VMEM((count, snaps), jnp.float32),
            pltpu.SemaphoreType.DMA((PROJECTION_STEPS,)),
            pltpu.SemaphoreType.DMA((PROJECTION_STEPS,)),
        ],
        compiler_params=pltpu.CompilerParams(vmem_limit_bytes=VMEM_LIMIT),
        cost_estimate=pl.CostEstimate(
            flops=2 * depth * count * snaps,
            bytes_accessed=2 * depth * (count + snaps),
            transcendentals=0,
        ),
    )(in_hbm(modes), in_hbm(snapshots))
    return [part.reshape((-1,) + exponent.shape) for part in parts], exponent[None]


def gram_kernel(sizes, turns, *refs):
    n_time, quarter, modes, row_block, col_block, target_block, tile = sizes
    half, snaps, is_last = n_time // 2, quarter * len(turns), 0 not in turns
    refs = list(refs)

    def taken(count):
        return [refs.pop(0) for _ in range(count)]

    pieces = taken(2 * len(turns))
    (before,) = taken(1) if is_last else (None,)
    outs = taken(2 if is_last else 1)
    lead, head, target, *rows, cols = taken(6)
    if is_last:
        (gram_hbm, rhs_hbm), (staged, side, side_staged, sems) = outs, refs
        scale = 1.0 / (n_time * QUAD * quarter)
    else:
        staged = side = outs[0]
        scale = 1.0
    aside = slice(0, target_block) if is_last else slice(col_block, col_block + target_block)
    later = (n_time - 1) * snaps
    time_pos, space_pos = lax.axis_index("tm"), lax.axis_index("space")
    core = lax.rem(time_pos, 2)

    def each_piece(take):
        for other in range(2):
            for k in range(half):
                block = jnp.bitwise_xor(time_pos, 2 * k + other)
                for j, turn in enumerate(turns):
                    source = partner(GATHER_PARTNERS, jnp.bitwise_xor(core, other), turn)
                    at = block * snaps + (source - min(turns)) * quarter
                    piece = pieces[other * len(turns) + j].at[k]
                    take(piece, pl.multiple_of(at, quarter))

    gap = 2 * snaps
    lead[:, 0:gap] = jnp.zeros((LEAD_MODES, gap), jnp.bfloat16)
    target[:, n_time * snaps :] = jnp.zeros((target_block, snaps), jnp.bfloat16)
    wanted = pl.ds(pl.multiple_of(space_pos * target_block, ROW_TILE), target_block)

    def place_lead(piece, at):
        current = piece[0:LEAD_MODES, :]
        head[:, pl.ds(at, quarter)] = current.astype(jnp.float32)
        lead[:, pl.ds(at + gap, quarter)] = current
        target[:, pl.ds(at, quarter)] = piece[wanted, :]

    each_piece(place_lead)

    def build_group(out, q, at):
        kind, i = lax.div(q, LEAD_MODES), lax.rem(q, LEAD_MODES)
        factor = jnp.broadcast_to(head[pl.ds(i, 1), snaps:], (ROW_TILE, later)).astype(
            jnp.bfloat16
        )
        shifted = pl.ds(pl.multiple_of(gap - kind * snaps, snaps), later)
        for j in range(0, LEAD_MODES, ROW_TILE):
            out[pl.ds(pl.multiple_of(at + j, ROW_TILE), ROW_TILE), snaps:] = (
                factor * lead[j : j + ROW_TILE, shifted]
            )

    def fill(out, start, extent):
        @pl.when(start == 0)
        def _():
            def place_modes(piece, at):
                out[pl.ds(LEAD_MODES, modes), pl.ds(at, quarter)] = piece[...]

            each_piece(place_modes)

        def group(q, carry):
            build_group(out, q, modes + LEAD_MODES * q - start + LEAD_MODES)
            return carry

        first = jnp.maximum(0, lax.div(start - modes, LEAD_MODES))
        last = lax.div(start + extent - modes + LEAD_MODES - 1, LEAD_MODES)
        lax.fori_loop(first, last, group, 0)

    def fill_products(out, start, extent):
        first = lax.div(start - modes, LEAD_MODES)
        most = 2 * LEAD_MODES - 1
        for g in range(-(-(extent + LEAD_MODES - ROW_TILE) // LEAD_MODES)):
            at = modes + LEAD_MODES * (first + g) - start + LEAD_MODES
            build_group(out, jnp.minimum(first + g, most), at)

    row_start = time_pos * row_block
    fill(cols, space_pos * col_block, col_block)
    fill(rows[0], row_start, tile)
    cols[pl.ds(LEAD_MODES + col_block, target_block), snaps:] = target[:, gap:]

    def times(left, right):
        return lax.dot_general(
            left, right, (((1,), (1,)), ((), ())), preferred_element_type=jnp.float32
        )

    first_rows = rows[0].at[pl.ds(LEAD_MODES, modes), 0:snaps]
    writes = []
    for step in range(row_block // tile):
        top = step * tile
        at = pl.ds(top, tile)
        if top + tile < row_block:
            fill_products(rows[(step + 1) % 2], row_start + top + tile, tile)
        product = times(
            rows[step % 2][pl.ds(LEAD_MODES, tile), snaps:],
            cols[pl.ds(LEAD_MODES, col_block + target_block), snaps:],
        )
        if is_last:
            product = (product + before[at, :]) * scale
        shape = (tile, col_block)
        row = time_pos * row_block + top + lax.broadcasted_iota(jnp.int32, shape, 0)
        column = space_pos * col_block + lax.broadcasted_iota(jnp.int32, shape, 1)
        if is_last:
            ridge = jnp.where(row == column, RIDGE_WEIGHT, 0.0)
            staged[at, :] = product[:, 0:col_block] + ridge
            side[at, :] = product[:, col_block:]
        else:
            staged[at, :] = product
        if step == 0:

            @pl.when((time_pos == 0) & (space_pos == 0))
            def _():
                end = LEAD_MODES + modes
                cols[end : end + target_block, 0:snaps] = target[:, snaps:gap]
                right = cols[LEAD_MODES : end + target_block, 0:snaps]
                extra = times(first_rows[...], right) * scale
                staged[0:modes, 0:modes] += extra[:, 0:modes]
                side[0:modes, aside] += extra[:, modes:]

            @pl.when((time_pos == 0) & (space_pos != 0))
            def _():
                extra = times(first_rows[...], target[:, snaps:gap]) * scale
                side[0:modes, aside] += extra

        if not is_last:
            continue
        writes.append(pltpu.make_async_copy(staged.at[at], gram_hbm.at[at], sems.at[step]))
        writes[-1].start()
    if not is_last:
        return
    side_staged[...] = side[...].T
    writes.append(pltpu.make_async_copy(side_staged, rhs_hbm, sems.at[len(writes)]))
    writes[-1].start()
    for write in writes:
        write.wait()


def add_quarters(turns, pieces, before, n_time, n_space):
    _, modes, quarter = pieces[0].shape
    features = modes + 2 * LEAD_MODES * LEAD_MODES
    row_block, col_block, target_block = features // n_time, features // n_space, modes // n_space
    tile = row_block // 4 if row_block % (4 * ROW_TILE) == 0 else row_block
    assert min(tile, col_block) >= modes
    snaps, is_last = quarter * len(turns), before is not None
    width = col_block + target_block
    total = n_time * snaps
    scratch = [
        pltpu.VMEM((LEAD_MODES, total + 2 * snaps), jnp.bfloat16),
        pltpu.VMEM((LEAD_MODES, total), jnp.float32),
        pltpu.VMEM((target_block, total + snaps), jnp.bfloat16),
        pltpu.VMEM((tile + 2 * LEAD_MODES, total), jnp.bfloat16),
        pltpu.VMEM((tile + 2 * LEAD_MODES, total), jnp.bfloat16),
        pltpu.VMEM((width + 2 * LEAD_MODES, total), jnp.bfloat16),
    ]
    vmem = pl.BlockSpec(memory_space=pltpu.VMEM)
    if is_last:
        out_shape = (
            jax.ShapeDtypeStruct((row_block, col_block), jnp.float32),
            jax.ShapeDtypeStruct((target_block, row_block), jnp.float32),
        )
        out_specs = (pl.BlockSpec(memory_space=pl.ANY),) * 2
        scratch += [
            pltpu.VMEM((row_block, col_block), jnp.float32),
            pltpu.VMEM((row_block, target_block), jnp.float32),
            pltpu.VMEM((target_block, row_block), jnp.float32),
            pltpu.SemaphoreType.DMA((row_block // tile + 1,)),
        ]
    else:
        out_shape, out_specs = pltpu.VMEM((row_block, width), jnp.float32), vmem
    operands = pieces + ([before] if is_last else [])
    return pl.pallas_call(
        functools.partial(
            gram_kernel,
            (n_time, quarter, modes, row_block, col_block, target_block, tile),
            turns,
        ),
        out_shape=out_shape,
        in_specs=[vmem] * len(operands),
        out_specs=out_specs,
        scratch_shapes=scratch,
        compiler_params=pltpu.CompilerParams(vmem_limit_bytes=GRAM_VMEM_LIMIT),
        cost_estimate=pl.CostEstimate(
            flops=EAGERNESS * row_block * width * total,
            bytes_accessed=4 * row_block * width,
            transcendentals=0,
        ),
    )(*map(in_vmem, operands))


def joined(value, axis, bit):
    return jnp.concatenate([value, swap(value, axis, bit)], axis=0)


def per_device(snapshots, modes):
    n_space, n_time = lax.axis_size("space"), lax.axis_size("tm")
    (mine, *others), exponent = project(modes, snapshots)
    arrived = [swap_quad(packed(part, exponent), SUM_PARTNERS, j) for j, part in enumerate(others, 1)]
    for part in arrived:
        value, scale = unpacked(part)
        mine, exponent = mine + value, jnp.maximum(exponent, scale)
    for bit in bits_of(n_space)[2:]:
        out = packed(mine, exponent)
        (mine, own), (value, scale) = unpacked(out), unpacked(swap(out, "space", bit))
        mine, exponent = mine + value, jnp.maximum(own, scale)
    mine = mine.astype(jnp.bfloat16).reshape(1, modes.shape[1], -1)
    for bit in bits_of(n_time)[1:]:
        mine = joined(mine, "tm", bit)
    others = [swap_quad(mine, GATHER_PARTNERS, j) for j in range(1, QUAD)]
    total = add_quarters((0,), [mine, swap(mine, "tm", 1)], None, n_time, n_space)
    pieces = others + [swap(piece, "tm", 1) for piece in others]
    gram, rhs = add_quarters((1, 2, 3), pieces, total, n_time, n_space)
    return gram, rhs.T


def solution(mesh):
    in_specs = (P("space", "tm"), P("space", None))
    out_specs = (P("tm", "space"), P("tm", "space"))
    return jax.shard_map(
        per_device, mesh=mesh, in_specs=in_specs, out_specs=out_specs, check_vma=False
    )
```

```python
import functools

import jax
import jax.numpy as jnp
from jax import lax
from jax.experimental import pallas as pl
from jax.experimental.pallas import tpu as pltpu
from jax.sharding import PartitionSpec as P

LEAD_MODES = 48
RIDGE_WEIGHT = 0.05
ROW_TILE = 16
QUAD = 4
SUM_PARTNERS = ((0, 3, 2, 1), (0, 3, 2, 1))
GATHER_PARTNERS = ((0, 2, 3, 1), (0, 3, 2, 1))
PROJECTION_STEPS = 16
EXPONENT_ROWS = 8
TOP = 9.0
SMALLEST = 1e-30
VMEM_LIMIT = 48 * 2**20
GRAM_VMEM_LIMIT = 32 * 2**20
EAGERNESS = 20


def swap(value, axis, bit):
    count = lax.axis_size(axis)
    return lax.ppermute(value, axis, [(i, i ^ bit) for i in range(count)])


def swap_quad(value, partners, turn):
    n_space, n_time = lax.axis_size("space"), lax.axis_size("tm")
    pairs = [
        (s * n_time + t, (s ^ partners[t % 2][turn]) * n_time + t)
        for s in range(n_space)
        for t in range(n_time)
    ]
    return lax.ppermute(value, ("space", "tm"), pairs)


def partner(partners, core, turn):
    even, odd = partners[0][turn], partners[1][turn]
    return even if even == odd else jnp.where(core == 0, even, odd)


def bits_of(count):
    return [1 << k for k in range(count.bit_length() - 1)]


def in_hbm(value):
    return pltpu.with_memory_space_constraint(value, pltpu.HBM)


def in_vmem(value):
    return pltpu.with_memory_space_constraint(value, pltpu.VMEM)


def packed(value, exponent):
    scaled = value * jnp.exp2(TOP - exponent)
    return jnp.concatenate([scaled, exponent], axis=0).astype(jnp.float16)


def unpacked(value):
    value = value.astype(jnp.float32)
    exponent = value[-1:]
    return value[0:-1] * jnp.exp2(exponent - TOP), exponent


def projection_kernel(modes_hbm, snaps_hbm, *refs):
    part_refs, exponent_ref = refs[0:QUAD], refs[QUAD]
    modes, snaps, partial_sums, modes_sems, snaps_sems = refs[QUAD + 1 :]
    depth = modes.shape[0] // PROJECTION_STEPS
    quarter = snaps.shape[1] // QUAD

    def copies(step):
        at = pl.ds(step * depth, depth)
        return (
            pltpu.make_async_copy(modes_hbm.at[at], modes.at[at], modes_sems.at[step]),
            pltpu.make_async_copy(snaps_hbm.at[at], snaps.at[at], snaps_sems.at[step]),
        )

    for step in range(PROJECTION_STEPS):
        for copy in copies(step):
            copy.start()
    for step in range(PROJECTION_STEPS):
        for copy in copies(step):
            copy.wait()
        at = pl.ds(step * depth, depth)
        product = lax.dot_general(
            modes[at, :],
            snaps[at, :],
            (((0,), (0,)), ((), ())),
            preferred_element_type=jnp.float32,
        )
        if step == 0:
            partial_sums[...] = product
        else:
            partial_sums[...] += product
    largest = jnp.maximum(jnp.max(jnp.abs(partial_sums[...])), SMALLEST)
    exponent_ref[...] = jnp.floor(jnp.log2(jnp.full(exponent_ref.shape, largest)))
    place = lax.rem(lax.axis_index("space"), QUAD)
    core = lax.rem(lax.axis_index("tm"), 2)
    for j in range(QUAD):
        start = pl.multiple_of(jnp.bitwise_xor(place, partner(SUM_PARTNERS, core, j)) * quarter, quarter)
        part_refs[j][...] = partial_sums[:, pl.ds(start, quarter)]


def project(modes, snapshots):
    (depth, count), snaps = modes.shape, snapshots.shape[1]
    quarter = snaps // QUAD
    vmem = pl.BlockSpec(memory_space=pltpu.VMEM)
    hbm = pl.BlockSpec(memory_space=pltpu.HBM)
    *parts, exponent = pl.pallas_call(
        projection_kernel,
        out_shape=(pltpu.VMEM((count, quarter), jnp.float32),) * QUAD
        + (pltpu.VMEM((EXPONENT_ROWS, quarter), jnp.float32),),
        in_specs=[hbm] * 2,
        out_specs=(vmem,) * (QUAD + 1),
        scratch_shapes=[
            pltpu.VMEM((depth, count), jnp.bfloat16),
            pltpu.VMEM((depth, snaps), jnp.bfloat16),
            pltpu.VMEM((count, snaps), jnp.float32),
            pltpu.SemaphoreType.DMA((PROJECTION_STEPS,)),
            pltpu.SemaphoreType.DMA((PROJECTION_STEPS,)),
        ],
        compiler_params=pltpu.CompilerParams(vmem_limit_bytes=VMEM_LIMIT),
        cost_estimate=pl.CostEstimate(
            flops=2 * depth * count * snaps,
            bytes_accessed=2 * depth * (count + snaps),
            transcendentals=0,
        ),
    )(in_hbm(modes), in_hbm(snapshots))
    return [part.reshape((-1,) + exponent.shape) for part in parts], exponent[None]


def gram_kernel(sizes, turns, *refs):
    n_time, quarter, modes, row_block, col_block, target_block, tile = sizes
    half, snaps, is_last = n_time // 2, quarter * len(turns), 0 not in turns
    refs = list(refs)

    def taken(count):
        return [refs.pop(0) for _ in range(count)]

    pieces = taken(2 * len(turns))
    (before,) = taken(1) if is_last else (None,)
    outs = taken(2 if is_last else 1)
    lead, head, target, *rows, cols = taken(6)
    if is_last:
        (gram_hbm, rhs_hbm), (staged, side, side_staged, sems) = outs, refs
        scale = 1.0 / (n_time * QUAD * quarter)
    else:
        staged = side = outs[0]
        scale = 1.0
    aside = slice(0, target_block) if is_last else slice(col_block, col_block + target_block)
    later = (n_time - 1) * snaps
    time_pos, space_pos = lax.axis_index("tm"), lax.axis_index("space")
    core = lax.rem(time_pos, 2)

    def each_piece(take):
        for other in range(2):
            for k in range(half):
                block = jnp.bitwise_xor(time_pos, 2 * k + other)
                for j, turn in enumerate(turns):
                    source = partner(GATHER_PARTNERS, jnp.bitwise_xor(core, other), turn)
                    at = block * snaps + (source - min(turns)) * quarter
                    piece = pieces[other * len(turns) + j].at[k]
                    take(piece, pl.multiple_of(at, quarter))

    gap = 2 * snaps
    lead[:, 0:gap] = jnp.zeros((LEAD_MODES, gap), jnp.bfloat16)
    target[:, n_time * snaps :] = jnp.zeros((target_block, snaps), jnp.bfloat16)
    wanted = pl.ds(pl.multiple_of(space_pos * target_block, ROW_TILE), target_block)

    def place_lead(piece, at):
        current = piece[0:LEAD_MODES, :]
        head[:, pl.ds(at, quarter)] = current.astype(jnp.float32)
        lead[:, pl.ds(at + gap, quarter)] = current
        target[:, pl.ds(at, quarter)] = piece[wanted, :]

    each_piece(place_lead)

    def build_group(out, q, at):
        kind, i = lax.div(q, LEAD_MODES), lax.rem(q, LEAD_MODES)
        factor = jnp.broadcast_to(head[pl.ds(i, 1), snaps:], (ROW_TILE, later)).astype(
            jnp.bfloat16
        )
        shifted = pl.ds(pl.multiple_of(gap - kind * snaps, snaps), later)
        for j in range(0, LEAD_MODES, ROW_TILE):
            out[pl.ds(pl.multiple_of(at + j, ROW_TILE), ROW_TILE), snaps:] = (
                factor * lead[j : j + ROW_TILE, shifted]
            )

    def fill(out, start, extent):
        @pl.when(start == 0)
        def _():
            def place_modes(piece, at):
                out[pl.ds(LEAD_MODES, modes), pl.ds(at, quarter)] = piece[...]

            each_piece(place_modes)

        def group(q, carry):
            build_group(out, q, modes + LEAD_MODES * q - start + LEAD_MODES)
            return carry

        first = jnp.maximum(0, lax.div(start - modes, LEAD_MODES))
        last = lax.div(start + extent - modes + LEAD_MODES - 1, LEAD_MODES)
        lax.fori_loop(first, last, group, 0)

    def fill_products(out, start, extent):
        first = lax.div(start - modes, LEAD_MODES)
        most = 2 * LEAD_MODES - 1
        for g in range(-(-(extent + LEAD_MODES - ROW_TILE) // LEAD_MODES)):
            at = modes + LEAD_MODES * (first + g) - start + LEAD_MODES
            build_group(out, jnp.minimum(first + g, most), at)

    row_start = time_pos * row_block
    fill(cols, space_pos * col_block, col_block)
    fill(rows[0], row_start, tile)
    cols[pl.ds(LEAD_MODES + col_block, target_block), snaps:] = target[:, gap:]

    def times(left, right):
        return lax.dot_general(
            left, right, (((1,), (1,)), ((), ())), preferred_element_type=jnp.float32
        )

    first_rows = rows[0].at[pl.ds(LEAD_MODES, modes), 0:snaps]
    writes = []
    for step in range(row_block // tile):
        top = step * tile
        at = pl.ds(top, tile)
        if top + tile < row_block:
            fill_products(rows[(step + 1) % 2], row_start + top + tile, tile)
        product = times(
            rows[step % 2][pl.ds(LEAD_MODES, tile), snaps:],
            cols[pl.ds(LEAD_MODES, col_block + target_block), snaps:],
        )
        if is_last:
            product = (product + before[at, :]) * scale
        shape = (tile, col_block)
        row = time_pos * row_block + top + lax.broadcasted_iota(jnp.int32, shape, 0)
        column = space_pos * col_block + lax.broadcasted_iota(jnp.int32, shape, 1)
        if is_last:
            ridge = jnp.where(row == column, RIDGE_WEIGHT, 0.0)
            staged[at, :] = product[:, 0:col_block] + ridge
            side[at, :] = product[:, col_block:]
        else:
            staged[at, :] = product
        if step == 0:

            @pl.when((time_pos == 0) & (space_pos == 0))
            def _():
                end = LEAD_MODES + modes
                cols[end : end + target_block, 0:snaps] = target[:, snaps:gap]
                right = cols[LEAD_MODES : end + target_block, 0:snaps]
                extra = times(first_rows[...], right) * scale
                staged[0:modes, 0:modes] += extra[:, 0:modes]
                side[0:modes, aside] += extra[:, modes:]

            @pl.when((time_pos == 0) & (space_pos != 0))
            def _():
                extra = times(first_rows[...], target[:, snaps:gap]) * scale
                side[0:modes, aside] += extra

        if not is_last:
            continue
        writes.append(pltpu.make_async_copy(staged.at[at], gram_hbm.at[at], sems.at[step]))
        writes[-1].start()
    if not is_last:
        return
    side_staged[...] = side[...].T
    writes.append(pltpu.make_async_copy(side_staged, rhs_hbm, sems.at[len(writes)]))
    writes[-1].start()
    for write in writes:
        write.wait()


def add_quarters(turns, pieces, before, n_time, n_space):
    _, modes, quarter = pieces[0].shape
    features = modes + 2 * LEAD_MODES * LEAD_MODES
    row_block, col_block, target_block = features // n_time, features // n_space, modes // n_space
    tile = row_block // 4 if row_block % (4 * ROW_TILE) == 0 else row_block
    assert min(tile, col_block) >= modes
    snaps, is_last = quarter * len(turns), before is not None
    width = col_block + target_block
    total = n_time * snaps
    scratch = [
        pltpu.VMEM((LEAD_MODES, total + 2 * snaps), jnp.bfloat16),
        pltpu.VMEM((LEAD_MODES, total), jnp.float32),
        pltpu.VMEM((target_block, total + snaps), jnp.bfloat16),
        pltpu.VMEM((tile + 2 * LEAD_MODES, total), jnp.bfloat16),
        pltpu.VMEM((tile + 2 * LEAD_MODES, total), jnp.bfloat16),
        pltpu.VMEM((width + 2 * LEAD_MODES, total), jnp.bfloat16),
    ]
    vmem = pl.BlockSpec(memory_space=pltpu.VMEM)
    if is_last:
        out_shape = (
            jax.ShapeDtypeStruct((row_block, col_block), jnp.float32),
            jax.ShapeDtypeStruct((target_block, row_block), jnp.float32),
        )
        out_specs = (pl.BlockSpec(memory_space=pl.ANY),) * 2
        scratch += [
            pltpu.VMEM((row_block, col_block), jnp.float32),
            pltpu.VMEM((row_block, target_block), jnp.float32),
            pltpu.VMEM((target_block, row_block), jnp.float32),
            pltpu.SemaphoreType.DMA((row_block // tile + 1,)),
        ]
    else:
        out_shape, out_specs = pltpu.VMEM((row_block, width), jnp.float32), vmem
    operands = pieces + ([before] if is_last else [])
    return pl.pallas_call(
        functools.partial(
            gram_kernel,
            (n_time, quarter, modes, row_block, col_block, target_block, tile),
            turns,
        ),
        out_shape=out_shape,
        in_specs=[vmem] * len(operands),
        out_specs=out_specs,
        scratch_shapes=scratch,
        compiler_params=pltpu.CompilerParams(vmem_limit_bytes=GRAM_VMEM_LIMIT),
        cost_estimate=pl.CostEstimate(
            flops=EAGERNESS * row_block * width * total,
            bytes_accessed=4 * row_block * width,
            transcendentals=0,
        ),
    )(*map(in_vmem, operands))


def joined(value, axis, bit):
    return jnp.concatenate([value, swap(value, axis, bit)], axis=0)


def per_device(snapshots, modes):
    n_space, n_time = lax.axis_size("space"), lax.axis_size("tm")
    (mine, *others), exponent = project(modes, snapshots)
    arrived = [swap_quad(packed(part, exponent), SUM_PARTNERS, j) for j, part in enumerate(others, 1)]
    for part in arrived:
        value, scale = unpacked(part)
        mine, exponent = mine + value, jnp.maximum(exponent, scale)
    for bit in bits_of(n_space)[2:]:
        out = packed(mine, exponent)
        (mine, own), (value, scale) = unpacked(out), unpacked(swap(out, "space", bit))
        mine, exponent = mine + value, jnp.maximum(own, scale)
    mine = mine.astype(jnp.bfloat16).reshape(1, modes.shape[1], -1)
    for bit in bits_of(n_time)[1:]:
        mine = joined(mine, "tm", bit)
    others = [swap_quad(mine, GATHER_PARTNERS, j) for j in range(1, QUAD)]
    total = add_quarters((0,), [mine, swap(mine, "tm", 1)], None, n_time, n_space)
    pieces = others + [swap(piece, "tm", 1) for piece in others]
    gram, rhs = add_quarters((1, 2, 3), pieces, total, n_time, n_space)
    return gram, rhs.T


def solution(mesh):
    in_specs = (P("space", "tm"), P("space", None))
    out_specs = (P("tm", "space"), P("tm", "space"))
    return jax.shard_map(
        per_device, mesh=mesh, in_specs=in_specs, out_specs=out_specs, check_vma=False
    )
```

```python
import functools

import jax
import jax.numpy as jnp
from jax import lax
from jax.experimental import pallas as pl
from jax.experimental.pallas import tpu as pltpu
from jax.sharding import PartitionSpec as P

LEAD_MODES = 48
RIDGE_WEIGHT = 0.05
ROW_TILE = 16
QUAD = 4
SUM_PARTNERS = ((0, 3, 2, 1), (0, 3, 2, 1))
GATHER_PARTNERS = ((0, 2, 3, 1), (0, 2, 3, 1))
PROJECTION_STEPS = 16
EXPONENT_ROWS = 8
TOP = 9.0
SMALLEST = 1e-30
VMEM_LIMIT = 48 * 2**20
GRAM_VMEM_LIMIT = 32 * 2**20
EAGERNESS = 20


def swap(value, axis, bit):
    count = lax.axis_size(axis)
    return lax.ppermute(value, axis, [(i, i ^ bit) for i in range(count)])


def swap_quad(value, partners, turn):
    n_space, n_time = lax.axis_size("space"), lax.axis_size("tm")
    pairs = [
        (s * n_time + t, (s ^ partners[t % 2][turn]) * n_time + t)
        for s in range(n_space)
        for t in range(n_time)
    ]
    return lax.ppermute(value, ("space", "tm"), pairs)


def partner(partners, core, turn):
    even, odd = partners[0][turn], partners[1][turn]
    return even if even == odd else jnp.where(core == 0, even, odd)


def bits_of(count):
    return [1 << k for k in range(count.bit_length() - 1)]


def in_hbm(value):
    return pltpu.with_memory_space_constraint(value, pltpu.HBM)


def in_vmem(value):
    return pltpu.with_memory_space_constraint(value, pltpu.VMEM)


def packed(value, exponent):
    scaled = value * jnp.exp2(TOP - exponent)
    return jnp.concatenate([scaled, exponent], axis=0).astype(jnp.float16)


def unpacked(value):
    value = value.astype(jnp.float32)
    exponent = value[-1:]
    return value[0:-1] * jnp.exp2(exponent - TOP), exponent


def projection_kernel(modes_hbm, snaps_hbm, *refs):
    part_refs, exponent_ref = refs[0:QUAD], refs[QUAD]
    modes, snaps, partial_sums, modes_sems, snaps_sems = refs[QUAD + 1 :]
    depth = modes.shape[0] // PROJECTION_STEPS
    quarter = snaps.shape[1] // QUAD

    def copies(step):
        at = pl.ds(step * depth, depth)
        return (
            pltpu.make_async_copy(modes_hbm.at[at], modes.at[at], modes_sems.at[step]),
            pltpu.make_async_copy(snaps_hbm.at[at], snaps.at[at], snaps_sems.at[step]),
        )

    for step in range(PROJECTION_STEPS):
        for copy in copies(step):
            copy.start()
    for step in range(PROJECTION_STEPS):
        for copy in copies(step):
            copy.wait()
        at = pl.ds(step * depth, depth)
        product = lax.dot_general(
            modes[at, :],
            snaps[at, :],
            (((0,), (0,)), ((), ())),
            preferred_element_type=jnp.float32,
        )
        if step == 0:
            partial_sums[...] = product
        else:
            partial_sums[...] += product
    largest = jnp.maximum(jnp.max(jnp.abs(partial_sums[...])), SMALLEST)
    exponent_ref[...] = jnp.floor(jnp.log2(jnp.full(exponent_ref.shape, largest)))
    place = lax.rem(lax.axis_index("space"), QUAD)
    core = lax.rem(lax.axis_index("tm"), 2)
    for j in range(QUAD):
        start = pl.multiple_of(jnp.bitwise_xor(place, partner(SUM_PARTNERS, core, j)) * quarter, quarter)
        part_refs[j][...] = partial_sums[:, pl.ds(start, quarter)]


def project(modes, snapshots):
    (depth, count), snaps = modes.shape, snapshots.shape[1]
    quarter = snaps // QUAD
    vmem = pl.BlockSpec(memory_space=pltpu.VMEM)
    hbm = pl.BlockSpec(memory_space=pltpu.HBM)
    *parts, exponent = pl.pallas_call(
        projection_kernel,
        out_shape=(pltpu.VMEM((count, quarter), jnp.float32),) * QUAD
        + (pltpu.VMEM((EXPONENT_ROWS, quarter), jnp.float32),),
        in_specs=[hbm] * 2,
        out_specs=(vmem,) * (QUAD + 1),
        scratch_shapes=[
            pltpu.VMEM((depth, count), jnp.bfloat16),
            pltpu.VMEM((depth, snaps), jnp.bfloat16),
            pltpu.VMEM((count, snaps), jnp.float32),
            pltpu.SemaphoreType.DMA((PROJECTION_STEPS,)),
            pltpu.SemaphoreType.DMA((PROJECTION_STEPS,)),
        ],
        compiler_params=pltpu.CompilerParams(vmem_limit_bytes=VMEM_LIMIT),
        cost_estimate=pl.CostEstimate(
            flops=2 * depth * count * snaps,
            bytes_accessed=2 * depth * (count + snaps),
            transcendentals=0,
        ),
    )(in_hbm(modes), in_hbm(snapshots))
    return [part.reshape((-1,) + exponent.shape) for part in parts], exponent[None]


def gram_kernel(sizes, turns, *refs):
    n_time, quarter, modes, row_block, col_block, target_block, tile = sizes
    half, snaps, is_last = n_time // 2, quarter * len(turns), 0 not in turns
    refs = list(refs)

    def taken(count):
        return [refs.pop(0) for _ in range(count)]

    pieces = taken(2 * len(turns))
    (before,) = taken(1) if is_last else (None,)
    outs = taken(2 if is_last else 1)
    lead, head, target, *rows, cols = taken(6)
    if is_last:
        (gram_hbm, rhs_hbm), (staged, side, side_staged, sems) = outs, refs
        scale = 1.0 / (n_time * QUAD * quarter)
    else:
        staged = side = outs[0]
        scale = 1.0
    aside = slice(0, target_block) if is_last else slice(col_block, col_block + target_block)
    later = (n_time - 1) * snaps
    time_pos, space_pos = lax.axis_index("tm"), lax.axis_index("space")
    core = lax.rem(time_pos, 2)

    def each_piece(take):
        for other in range(2):
            for k in range(half):
                block = jnp.bitwise_xor(time_pos, 2 * k + other)
                for j, turn in enumerate(turns):
                    source = partner(GATHER_PARTNERS, jnp.bitwise_xor(core, other), turn)
                    at = block * snaps + (source - min(turns)) * quarter
                    piece = pieces[other * len(turns) + j].at[k]
                    take(piece, pl.multiple_of(at, quarter))

    gap = 2 * snaps
    lead[:, 0:gap] = jnp.zeros((LEAD_MODES, gap), jnp.bfloat16)
    target[:, n_time * snaps :] = jnp.zeros((target_block, snaps), jnp.bfloat16)
    wanted = pl.ds(pl.multiple_of(space_pos * target_block, ROW_TILE), target_block)

    def place_lead(piece, at):
        current = piece[0:LEAD_MODES, :]
        head[:, pl.ds(at, quarter)] = current.astype(jnp.float32)
        lead[:, pl.ds(at + gap, quarter)] = current
        target[:, pl.ds(at, quarter)] = piece[wanted, :]

    each_piece(place_lead)

    def build_group(out, q, at):
        kind, i = lax.div(q, LEAD_MODES), lax.rem(q, LEAD_MODES)
        factor = jnp.broadcast_to(head[pl.ds(i, 1), snaps:], (ROW_TILE, later)).astype(
            jnp.bfloat16
        )
        shifted = pl.ds(pl.multiple_of(gap - kind * snaps, snaps), later)
        for j in range(0, LEAD_MODES, ROW_TILE):
            out[pl.ds(pl.multiple_of(at + j, ROW_TILE), ROW_TILE), snaps:] = (
                factor * lead[j : j + ROW_TILE, shifted]
            )

    def fill(out, start, extent):
        @pl.when(start == 0)
        def _():
            def place_modes(piece, at):
                out[pl.ds(LEAD_MODES, modes), pl.ds(at, quarter)] = piece[...]

            each_piece(place_modes)

        def group(q, carry):
            build_group(out, q, modes + LEAD_MODES * q - start + LEAD_MODES)
            return carry

        first = jnp.maximum(0, lax.div(start - modes, LEAD_MODES))
        last = lax.div(start + extent - modes + LEAD_MODES - 1, LEAD_MODES)
        lax.fori_loop(first, last, group, 0)

    def fill_products(out, start, extent):
        first = lax.div(start - modes, LEAD_MODES)
        most = 2 * LEAD_MODES - 1
        for g in range(-(-(extent + LEAD_MODES - ROW_TILE) // LEAD_MODES)):
            at = modes + LEAD_MODES * (first + g) - start + LEAD_MODES
            build_group(out, jnp.minimum(first + g, most), at)

    row_start = time_pos * row_block
    fill(cols, space_pos * col_block, col_block)
    fill(rows[0], row_start, tile)
    cols[pl.ds(LEAD_MODES + col_block, target_block), snaps:] = target[:, gap:]

    def times(left, right):
        return lax.dot_general(
            left, right, (((1,), (1,)), ((), ())), preferred_element_type=jnp.float32
        )

    first_rows = rows[0].at[pl.ds(LEAD_MODES, modes), 0:snaps]
    writes = []
    for step in range(row_block // tile):
        top = step * tile
        at = pl.ds(top, tile)
        if top + tile < row_block:
            fill_products(rows[(step + 1) % 2], row_start + top + tile, tile)
        product = times(
            rows[step % 2][pl.ds(LEAD_MODES, tile), snaps:],
            cols[pl.ds(LEAD_MODES, col_block + target_block), snaps:],
        )
        if is_last:
            product = (product + before[at, :]) * scale
        shape = (tile, col_block)
        row = time_pos * row_block + top + lax.broadcasted_iota(jnp.int32, shape, 0)
        column = space_pos * col_block + lax.broadcasted_iota(jnp.int32, shape, 1)
        if is_last:
            ridge = jnp.where(row == column, RIDGE_WEIGHT, 0.0)
            staged[at, :] = product[:, 0:col_block] + ridge
            side[at, :] = product[:, col_block:]
        else:
            staged[at, :] = product
        if step == 0:

            @pl.when((time_pos == 0) & (space_pos == 0))
            def _():
                end = LEAD_MODES + modes
                cols[end : end + target_block, 0:snaps] = target[:, snaps:gap]
                right = cols[LEAD_MODES : end + target_block, 0:snaps]
                extra = times(first_rows[...], right) * scale
                staged[0:modes, 0:modes] += extra[:, 0:modes]
                side[0:modes, aside] += extra[:, modes:]

            @pl.when((time_pos == 0) & (space_pos != 0))
            def _():
                extra = times(first_rows[...], target[:, snaps:gap]) * scale
                side[0:modes, aside] += extra

        if not is_last:
            continue
        writes.append(pltpu.make_async_copy(staged.at[at], gram_hbm.at[at], sems.at[step]))
        writes[-1].start()
    if not is_last:
        return
    side_staged[...] = side[...].T
    writes.append(pltpu.make_async_copy(side_staged, rhs_hbm, sems.at[len(writes)]))
    writes[-1].start()
    for write in writes:
        write.wait()


def add_quarters(turns, pieces, before, n_time, n_space):
    _, modes, quarter = pieces[0].shape
    features = modes + 2 * LEAD_MODES * LEAD_MODES
    row_block, col_block, target_block = features // n_time, features // n_space, modes // n_space
    tile = row_block // 4 if row_block % (4 * ROW_TILE) == 0 else row_block
    assert min(tile, col_block) >= modes
    snaps, is_last = quarter * len(turns), before is not None
    width = col_block + target_block
    total = n_time * snaps
    scratch = [
        pltpu.VMEM((LEAD_MODES, total + 2 * snaps), jnp.bfloat16),
        pltpu.VMEM((LEAD_MODES, total), jnp.float32),
        pltpu.VMEM((target_block, total + snaps), jnp.bfloat16),
        pltpu.VMEM((tile + 2 * LEAD_MODES, total), jnp.bfloat16),
        pltpu.VMEM((tile + 2 * LEAD_MODES, total), jnp.bfloat16),
        pltpu.VMEM((width + 2 * LEAD_MODES, total), jnp.bfloat16),
    ]
    vmem = pl.BlockSpec(memory_space=pltpu.VMEM)
    if is_last:
        out_shape = (
            jax.ShapeDtypeStruct((row_block, col_block), jnp.float32),
            jax.ShapeDtypeStruct((target_block, row_block), jnp.float32),
        )
        out_specs = (pl.BlockSpec(memory_space=pl.ANY),) * 2
        scratch += [
            pltpu.VMEM((row_block, col_block), jnp.float32),
            pltpu.VMEM((row_block, target_block), jnp.float32),
            pltpu.VMEM((target_block, row_block), jnp.float32),
            pltpu.SemaphoreType.DMA((row_block // tile + 1,)),
        ]
    else:
        out_shape, out_specs = pltpu.VMEM((row_block, width), jnp.float32), vmem
    operands = pieces + ([before] if is_last else [])
    return pl.pallas_call(
        functools.partial(
            gram_kernel,
            (n_time, quarter, modes, row_block, col_block, target_block, tile),
            turns,
        ),
        out_shape=out_shape,
        in_specs=[vmem] * len(operands),
        out_specs=out_specs,
        scratch_shapes=scratch,
        compiler_params=pltpu.CompilerParams(vmem_limit_bytes=GRAM_VMEM_LIMIT),
        cost_estimate=pl.CostEstimate(
            flops=EAGERNESS * row_block * width * total,
            bytes_accessed=4 * row_block * width,
            transcendentals=0,
        ),
    )(*map(in_vmem, operands))


def joined(value, axis, bit):
    return jnp.concatenate([value, swap(value, axis, bit)], axis=0)


def per_device(snapshots, modes):
    n_space, n_time = lax.axis_size("space"), lax.axis_size("tm")
    (mine, *others), exponent = project(modes, snapshots)
    arrived = [swap_quad(packed(part, exponent), SUM_PARTNERS, j) for j, part in enumerate(others, 1)]
    for part in arrived:
        value, scale = unpacked(part)
        mine, exponent = mine + value, jnp.maximum(exponent, scale)
    for bit in bits_of(n_space)[2:]:
        out = packed(mine, exponent)
        (mine, own), (value, scale) = unpacked(out), unpacked(swap(out, "space", bit))
        mine, exponent = mine + value, jnp.maximum(own, scale)
    mine = mine.astype(jnp.bfloat16).reshape(1, modes.shape[1], -1)
    for bit in bits_of(n_time)[1:]:
        mine = joined(mine, "tm", bit)
    others = [swap_quad(mine, GATHER_PARTNERS, j) for j in range(1, QUAD)]
    total = add_quarters((0,), [mine, swap(mine, "tm", 1)], None, n_time, n_space)
    pieces = others + [swap(piece, "tm", 1) for piece in others]
    gram, rhs = add_quarters((1, 2, 3), pieces, total, n_time, n_space)
    return gram, rhs.T


def solution(mesh):
    in_specs = (P("space", "tm"), P("space", None))
    out_specs = (P("tm", "space"), P("tm", "space"))
    return jax.shard_map(
        per_device, mesh=mesh, in_specs=in_specs, out_specs=out_specs, check_vma=False
    )
```
